32 devices in a mesh: acq: 8 (over y, x, core), rcv: 4 (over z).
Axes of the slice: x: 2, y: 2, z: 4, core: 2. Of those that a mesh axis runs over, the one named last changes fastest.
Arguments:
- raw_blocks: bfloat16 [32, 1024, 512], P('acq', None, 'rcv'), may hold values from -6 to 6
- raw_dest: int32 [32], P('acq'), may hold values from 0 to 7, as said below
- raw_count: int32 [8], P('acq'), may hold values from 2 to 4, as said below
- stencil: int32 [512, 2], P('acq'), may hold values from 0 to 7, as said below
- stencil_weight: bfloat16 [512, 2], P('acq'), may hold values from 0.25 to 1
- kernel: bfloat16 [2, 2, 384], replicated, may hold values from -0.25 to 0.25
Outputs:
- multiples: bfloat16 [2, 512, 4, 2, 128], P(None, 'acq', 'rcv')
The draws below stay inside these ranges and needn't reach their ends.
Inputs may be any that keep to these rules, and one draw needn't show every extreme that they name: `raw_dest`: within one group the 4 blocks go to different owners, so at most 1 to any owner, and every group reaches that; the first 2 blocks of group a go to the owners congruent to a modulo 4. `raw_count`: some group uses all 4 of its blocks. `stencil`: each row names two different slots of its owner's slot table that are filled by an in-use block.
All inputs are finite; a program needn't handle non-finite values.
Results may differ from the reference program's by a relative error of at most 0.0061.
Values may be sent and summed in bfloat16 or wider, within the bound.
A program may use at most 64 MiB of HBM per device.

```python
import math
import jax
import jax.numpy as jnp
from jax import lax

NT = 1024
PK = 128
SHOT_DEV = 64
NF = 2
FLO = 32
CAP = 1
RAW_DEV = 4
SLOTS = 8
RAW_ALL = 32
SHOTS = 512
POINTS = 512
STOPS = 2
KLEN = 384
N_ACQ = 8
N_RCV = 4


def routing(key):
    key_count, key_group, key_near, distant_key = jax.random.split(jax.random.fold_in(key, 7), 4)
    quarter = N_ACQ // 4
    counts = jax.random.randint(key_count, (N_ACQ,), RAW_DEV // 2, RAW_DEV + 1)
    full_group = jax.random.randint(key_group, (), 0, N_ACQ)
    counts = jnp.where(jnp.arange(N_ACQ) == full_group, RAW_DEV, counts).astype(jnp.int32)
    group_ids = jnp.arange(N_ACQ)[:, None]
    near_order = jax.vmap(lambda group_key: jax.random.permutation(group_key, quarter))(jax.random.split(key_near, N_ACQ))
    near_dest = (group_ids + 4 * near_order) % N_ACQ
    far_order = jax.vmap(lambda group_key: jax.random.permutation(group_key, 3 * quarter))(jax.random.split(distant_key, N_ACQ))[:, :quarter]
    far_dest = (group_ids + 4 * (far_order % quarter) + 1 + far_order // quarter) % N_ACQ
    dest_list = jnp.concatenate([near_dest, far_dest], axis=1)
    return (counts, dest_list.astype(jnp.int32))


def draw_raw_dest(key, part):
    return routing(key)[1].reshape(-1)


def draw_raw_count(key, part):
    return routing(key)[0]


def draw_stencil(key, part):
    counts, dest_list = routing(key)
    is_live = jnp.arange(RAW_DEV)[None, :] < counts[:, None]
    sent_count = jnp.sum((dest_list[:, :, None] == jnp.arange(N_ACQ)[None, None, :]) & is_live[:, :, None], axis=1)
    slot_live = jnp.arange(CAP)[None, None, :] < sent_count[:, :, None]
    live_table = jnp.transpose(slot_live, (1, 0, 2)).reshape(N_ACQ, SLOTS)
    shot_holder = jnp.arange(SHOTS) // SHOT_DEV
    usable = live_table[shot_holder]
    scores = jax.random.randint(jax.random.fold_in(key, 11), (SHOTS, SLOTS), 0, 4096) * SLOTS + jnp.arange(SLOTS)[None, :]
    scores = jnp.where(usable, scores, -1)
    top_values, chosen = lax.top_k(scores, 2)
    return chosen.astype(jnp.int32)


def levels(key, dims, shards, smallest, top_value):
    def one(axis_at, parts):
        draws = jax.random.uniform(jax.random.fold_in(jax.random.fold_in(key, 6), axis_at), (parts,), jnp.float32, smallest / len(shards), top_value / len(shards))
        return jnp.repeat(jnp.exp(draws), dims[axis_at] // parts).reshape((-1,) + (1,) * (len(dims) - axis_at - 1))

    factor_of = one(*shards[0])
    for cut in shards[1:]:
        factor_of = factor_of * one(*cut)
    return factor_of


def noise(own_key, dims, deviation, most, cuts=(), kind=jnp.bfloat16):
    drawn = deviation * jax.random.normal(own_key, dims, jnp.float32)
    if cuts:
        drawn = drawn * levels(own_key, dims, cuts, -0.22, 0.18)
    return jnp.clip(drawn, -most, most).astype(kind)


def setup_inputs(seed: int = 0) -> dict:
    seeds = jax.random.split(jax.random.key(seed), 7)
    raw_blocks = noise(seeds[0], (RAW_ALL, NT, POINTS), 1.0, 6.0, ((0, 8), (2, 4)))
    raw_dest = draw_raw_dest(jax.random.fold_in(seeds[6], 71), 0)
    raw_count = draw_raw_count(jax.random.fold_in(seeds[6], 71), 0)
    stencil = draw_stencil(jax.random.fold_in(seeds[6], 71), 0)
    stencil_weight = jnp.clip(0.25 + 0.75 * jax.random.uniform(seeds[4], (SHOTS, 2), jnp.float32) ** levels(seeds[4], (SHOTS, 2), ((0, 8),), -0.2, 0.2), 0.25, 1.0).astype(jnp.bfloat16)
    kernel = noise(seeds[5], (NF, 2, KLEN), (2 * STOPS * PK) ** -0.5, 0.25)
    return dict(raw_blocks=raw_blocks, raw_dest=raw_dest, raw_count=raw_count, stencil=stencil, stencil_weight=stencil_weight, kernel=kernel)


def dft_table(freq_count, sample_count):
    freqs = FLO + jnp.arange(freq_count, dtype=jnp.int32)
    samples = jnp.arange(sample_count, dtype=jnp.int32)
    angles = (freqs[:, None] * samples[None, :] % sample_count).astype(jnp.float32) * (2.0 * math.pi / sample_count)
    cosines = jnp.stack([jnp.cos(angles), -jnp.sin(angles)], axis=1) / math.sqrt(sample_count)
    return cosines.reshape(2 * freq_count, sample_count).astype(jnp.bfloat16)

def block_operator(kernel, offset, stop_count, panel_width):
    shot_positions = (offset + stop_count // 2) * panel_width + jnp.arange(panel_width, dtype=jnp.int32)[:, None] - jnp.arange(panel_width, dtype=jnp.int32)[None, :]
    entries = jnp.take(kernel, shot_positions, axis=2)
    real_component = entries[:, 0]
    imag_part = entries[:, 1]
    upper_rows = jnp.concatenate([real_component, imag_part], axis=-1)
    lower_rows = jnp.concatenate([-imag_part, real_component], axis=-1)
    return jnp.concatenate([upper_rows, lower_rows], axis=1)

def reference(raw_blocks, raw_dest, raw_count, stencil, stencil_weight, kernel):
    fourier_rows = dft_table(NF, NT).astype(jnp.float32)
    grouped = raw_blocks.reshape(N_ACQ, RAW_DEV, NT, POINTS)

    def transform(blocks):
        return jnp.einsum('gt,jtp->jgp', fourier_rows, blocks.astype(jnp.float32)).astype(jnp.bfloat16)
    spectra = lax.map(transform, grouped)
    dest_list = raw_dest.reshape(N_ACQ, RAW_DEV)
    is_live = jnp.arange(RAW_DEV, dtype=jnp.int32)[None, :] < raw_count[:, None]
    onehot = ((dest_list[:, :, None] == jnp.arange(N_ACQ, dtype=jnp.int32)[None, None, :]) & is_live[:, :, None]).astype(jnp.int32)
    slot_rank = lax.optimization_barrier(jnp.sum(jnp.cumsum(onehot, axis=1) * onehot, axis=2)) - 1
    target = jnp.where(is_live, dest_list * SLOTS + jnp.arange(N_ACQ, dtype=jnp.int32)[:, None] * CAP + slot_rank, N_ACQ * SLOTS).astype(jnp.int32)
    slot_rows = jnp.zeros((N_ACQ * SLOTS, 2 * NF, POINTS), jnp.bfloat16)
    slot_rows = slot_rows.at[target.reshape(-1)].set(spectra.reshape(-1, 2 * NF, POINTS), mode='drop')
    slot_groups = slot_rows.reshape(N_ACQ, SLOTS, 2 * NF, POINTS)
    stencil_groups = stencil.reshape(N_ACQ, SHOT_DEV, 2)
    weight_groups = stencil_weight.astype(jnp.float32).reshape(N_ACQ, SHOT_DEV, 2)

    def interpolate(items):
        owned_rows, chosen, weights = items
        first = owned_rows[chosen[:, 0]].astype(jnp.float32)
        second = owned_rows[chosen[:, 1]].astype(jnp.float32)
        return (weights[:, 0, None, None] * first + weights[:, 1, None, None] * second).astype(jnp.bfloat16)
    regular = lax.map(interpolate, (slot_groups, stencil_groups, weight_groups)).reshape(SHOTS, NF, 2, N_RCV, PK)
    panels = regular.transpose(1, 0, 3, 2, 4).reshape(NF, SHOTS, N_RCV, 2 * PK)

    def one_freq(items):
        receiver_panel, kern = items
        running_totals = jnp.zeros((SHOTS, N_RCV, 2 * PK), jnp.float32)
        for offset in range(-(STOPS // 2 - 1), STOPS // 2 + 1):
            prediction_operator = block_operator(kern[None], offset, STOPS, PK)[0].astype(jnp.float32)
            rolled = jnp.roll(receiver_panel, -offset, axis=1).astype(jnp.float32)
            running_totals = running_totals + jnp.einsum('sik,kr->sir', rolled, prediction_operator)
        return running_totals.astype(jnp.bfloat16)
    multiples = lax.map(one_freq, (panels, kernel))
    return multiples.reshape(NF, SHOTS, N_RCV, 2, PK)
```

```python
import functools
import math

import jax
import jax.numpy as jnp
import numpy as np
from jax import lax
from jax.experimental import pallas as pl
from jax.experimental.pallas import tpu as pltpu
from jax.sharding import PartitionSpec as P

FLO = 32
MESH = pl.DeviceIdType.MESH
F32 = jnp.float32
BF16 = jnp.bfloat16


def dft_table(freq_count, sample_count, row_count):
    freqs = FLO + np.arange(freq_count, dtype=np.int32)
    samples = np.arange(sample_count, dtype=np.int32)
    angles = (freqs[:, None] * samples[None, :] % sample_count).astype(np.float32) * np.float32(
        2.0 * math.pi / sample_count
    )
    rows = np.stack([np.cos(angles), -np.sin(angles)], axis=1) / np.float32(math.sqrt(sample_count))
    table = np.zeros((row_count, sample_count), np.float32)
    table[: 2 * freq_count] = rows.reshape(2 * freq_count, sample_count)
    return jnp.asarray(table, BF16)


def kernel(
    groups, panels, stops,
    table_hbm, raw_hbm, dest_hbm, count_hbm, stencil_hbm, weight_hbm, kern_hbm,
    out_ref,
    table, raw, dest, count, stencil, weight, kern, packed, received, slots, operator,
    raw_sems, small_sems, send_sem, recv_sems,
):
    raw_slots = raw.shape[0]
    rows = packed.shape[1]
    freq_count = rows // 2
    padded = slots.shape[0] // groups
    width = raw.shape[2]
    shot_count = stencil.shape[1]
    back_reach = stops // 2 - 1
    my_group = lax.axis_index("acq")
    my_panel = lax.axis_index("rcv")

    small = [
        pltpu.make_async_copy(src, dst, small_sems.at[at])
        for at, (src, dst) in enumerate([
            (table_hbm, table), (dest_hbm, dest), (count_hbm, count),
            (stencil_hbm, stencil), (weight_hbm, weight), (kern_hbm, kern),
        ])
    ]
    loads = [
        pltpu.make_async_copy(raw_hbm.at[j], raw.at[j], raw_sems.at[j]) for j in range(raw_slots)
    ]
    small[0].start()
    for load in loads:
        load.start()
    for copy in small[1:]:
        copy.start()

    def peers():
        for stop in range(stops):
            for step in range(groups):
                if stop != back_reach or step != 0:
                    yield stop, stop - back_reach, lax.rem(my_group + step, groups)

    barrier = pltpu.get_barrier_semaphore()
    for _, offset, group in peers():
        pl.semaphore_signal(
            barrier, inc=1,
            device_id={"acq": group, "rcv": lax.rem(my_panel + offset + panels, panels)},
            device_id_type=MESH,
        )

    small[0].wait()
    small[1].wait()
    small[2].wait()
    spectra = []
    for first in range(0, raw_slots, 2):
        blocks = list(range(first, min(first + 2, raw_slots)))
        for j in blocks:
            loads[j].wait()
        pair = jnp.concatenate([raw[j] for j in blocks], axis=1)
        both = jnp.dot(table[...], pair, preferred_element_type=F32)
        both = both.astype(BF16).astype(F32)
        for at in range(len(blocks)):
            spectra.append(both[:rows, at * width:(at + 1) * width])
    slot_of = [jnp.where(j < count[0], dest[j], -1) for j in range(raw_slots)]
    for owner in range(groups):
        total = jnp.zeros((rows, width), F32)
        for j in range(raw_slots):
            total = total + jnp.where(slot_of[j] == owner, 1.0, 0.0) * spectra[j]
        packed[owner] = total.astype(BF16)

    pl.semaphore_wait(barrier, groups * stops - 1)
    for stop, offset, group in peers():
        pltpu.make_async_remote_copy(
            src_ref=packed.at[group],
            dst_ref=received.at[stop, my_group],
            send_sem=send_sem,
            recv_sem=recv_sems.at[stop],
            device_id={"acq": group, "rcv": lax.rem(my_panel - offset + panels, panels)},
            device_id_type=MESH,
        ).start()
    received[back_reach, my_group] = packed[my_group]

    for copy in small[3:]:
        copy.wait()
    slots[...] = jnp.zeros_like(slots)
    lane = lax.broadcasted_iota(jnp.int32, (width, width), 1)
    row = lax.broadcasted_iota(jnp.int32, (width, width), 0)
    for f in range(freq_count):
        for c in range(2):
            line = kern[f, c:c + 1, :].astype(F32)
            if c == 1:
                line = -line
            rolled = [
                pltpu.roll(
                    jnp.broadcast_to(line[:, at * width:(at + 1) * width], (width, width)),
                    0, 1, stride=1, stride_axis=0,
                )
                for at in range(stops + 1)
            ]
            for stop in range(stops):
                place = (2 * stop + c) * width
                operator[f, :, place:place + width] = jnp.where(
                    lane >= row, rolled[stop + 1], rolled[stop]
                ).astype(BF16)

    slot_at = lax.broadcasted_iota(jnp.int32, (groups * padded, shot_count), 0) // padded
    weights = weight[...].astype(F32)
    mixing = jnp.where(slot_at == stencil[0:1, :], weights[0:1, :], 0.0)
    mixing = mixing + jnp.where(slot_at == stencil[1:2, :], weights[1:2, :], 0.0)
    spread_rows = lax.broadcasted_iota(jnp.int32, (2 * shot_count, shot_count), 0)
    spread_cols = lax.broadcasted_iota(jnp.int32, (2 * shot_count, shot_count), 1)
    spread = jnp.where(spread_rows // 2 == spread_cols, 1.0, 0.0).astype(BF16)
    mixing = lax.dot_general(
        spread, mixing.astype(BF16), (((1,), (1,)), ((), ())), preferred_element_type=F32
    )
    part = lax.broadcasted_iota(jnp.int32, mixing.shape, 0) % 2
    component = lax.broadcasted_iota(jnp.int32, mixing.shape, 1) % padded
    mixers = []
    for f in range(freq_count):
        mixers.append(jnp.where(component == 2 * f + part, mixing, 0.0).astype(BF16))
        signed = jnp.where(part == 0, mixing, -mixing)
        mixers.append(jnp.where(component == 2 * f + 1 - part, signed, 0.0).astype(BF16))
    mixers = jnp.concatenate(mixers, axis=0)

    for stop in range(stops):
        arrived = received.at[stop]
        if stop == back_reach:
            arrived = received.at[stop, pl.ds(0, groups - 1)]
        pltpu.make_async_copy(arrived, arrived, recv_sems.at[stop]).wait()
        for group in range(groups):
            slots[group * padded:group * padded + rows, stop * width:(stop + 1) * width] = (
                received[stop, group].astype(F32)
            )
    regular = jnp.dot(mixers, slots[...].astype(BF16), preferred_element_type=F32).astype(BF16)
    pairs = 2 * shot_count
    for f in range(freq_count):
        fields = []
        for stop in range(stops):
            for c in range(2):
                at = (2 * f + c) * pairs
                fields.append(regular[at:at + pairs, stop * width:(stop + 1) * width])
        fields = jnp.concatenate(fields, axis=1)
        out_ref[f] = lax.dot_general(
            fields, operator[f], (((1,), (1,)), ((), ())), preferred_element_type=F32
        ).astype(BF16)

    for stop in range(stops):
        sent = packed
        if stop == back_reach:
            sent = packed.at[pl.ds(0, groups - 1)]
        pltpu.make_async_copy(sent, sent, send_sem).wait()


def shards(raw_blocks, raw_dest, raw_count, stencil, stencil_weight, kern):
    groups = lax.axis_size("acq")
    panels = lax.axis_size("rcv")
    stops = panels // 2
    raw_slots, sample_count, width = raw_blocks.shape
    freq_count = kern.shape[0]
    shot_count = stencil.shape[0]
    rows = 2 * freq_count
    padded = -(-rows // 8) * 8
    table = dft_table(freq_count, sample_count, -(-rows // 16) * 16)
    out = pl.pallas_call(
        functools.partial(kernel, groups, panels, stops),
        out_shape=jax.ShapeDtypeStruct((freq_count, 2 * shot_count, width), BF16),
        in_specs=[pl.BlockSpec(memory_space=pl.ANY)] * 7,
        out_specs=pl.BlockSpec(memory_space=pltpu.VMEM),
        scratch_shapes=[
            pltpu.VMEM(table.shape, BF16),
            pltpu.VMEM(raw_blocks.shape, BF16),
            pltpu.SMEM(raw_dest.shape, jnp.int32),
            pltpu.SMEM(raw_count.shape, jnp.int32),
            pltpu.VMEM((2, shot_count), jnp.int32),
            pltpu.VMEM((2, shot_count), BF16),
            pltpu.VMEM(kern.shape, BF16),
            pltpu.VMEM((groups, rows, width), BF16),
            pltpu.VMEM((stops, groups, rows, width), BF16),
            pltpu.VMEM((groups * padded, stops * width), F32),
            pltpu.VMEM((freq_count, width, 2 * stops * width), BF16),
            pltpu.SemaphoreType.DMA((raw_slots,)),
            pltpu.SemaphoreType.DMA((6,)),
            pltpu.SemaphoreType.DMA,
            pltpu.SemaphoreType.DMA((stops,)),
        ],
        compiler_params=pltpu.CompilerParams(
            collective_id=0, has_side_effects=True, vmem_limit_bytes=60 * 1024 * 1024
        ),
    )(table, raw_blocks, raw_dest, raw_count, stencil.T, stencil_weight.T, kern)
    return out.reshape(freq_count, shot_count, 1, 2, width)


def solution(mesh):
    return jax.shard_map(
        shards,
        mesh=mesh,
        in_specs=(P("acq", None, "rcv"), P("acq"), P("acq"), P("acq", None), P("acq", None), P()),
        out_specs=P(None, "acq", "rcv", None, None),
        check_vma=False,
    )
```

```python
import functools
import math

import jax
import jax.numpy as jnp
import numpy as np
from jax import lax
from jax.experimental import pallas as pl
from jax.experimental.pallas import tpu as pltpu
from jax.sharding import PartitionSpec as P

FLO = 32
MESH = pl.DeviceIdType.MESH
F32 = jnp.float32
BF16 = jnp.bfloat16


def dft_table(freq_count, sample_count, row_count):
    freqs = FLO + np.arange(freq_count, dtype=np.int32)
    samples = np.arange(sample_count, dtype=np.int32)
    angles = (freqs[:, None] * samples[None, :] % sample_count).astype(np.float32) * np.float32(
        2.0 * math.pi / sample_count
    )
    rows = np.stack([np.cos(angles), -np.sin(angles)], axis=1) / np.float32(math.sqrt(sample_count))
    table = np.zeros((row_count, sample_count), np.float32)
    table[: 2 * freq_count] = rows.reshape(2 * freq_count, sample_count)
    return jnp.asarray(table, BF16)


def kernel(
    groups, panels, stops,
    table_hbm, raw_hbm, dest_hbm, count_hbm, stencil_hbm, weight_hbm, kern_hbm,
    out_ref,
    table, raw, dest, count, stencil, weight, kern, packed, received, slots, operator,
    raw_sems, small_sems, send_sem, recv_sems,
):
    raw_slots = raw.shape[0]
    rows = packed.shape[1]
    freq_count = rows // 2
    padded = slots.shape[1] // groups
    width = raw.shape[2]
    shot_count = stencil.shape[1]
    back_reach = stops // 2 - 1
    my_group = lax.axis_index("acq")
    my_panel = lax.axis_index("rcv")

    small = [
        pltpu.make_async_copy(src, dst, small_sems.at[at])
        for at, (src, dst) in enumerate([
            (table_hbm, table), (dest_hbm, dest), (count_hbm, count),
            (stencil_hbm, stencil), (weight_hbm, weight), (kern_hbm, kern),
        ])
    ]
    loads = [
        pltpu.make_async_copy(raw_hbm.at[j], raw.at[j], raw_sems.at[j]) for j in range(raw_slots)
    ]
    small[0].start()
    for load in loads:
        load.start()
    for copy in small[1:]:
        copy.start()

    def moved(place, by, count):
        place = place + by
        if by < 0:
            return jnp.where(place < 0, place + count, place)
        return jnp.where(place >= count, place - count, place)

    far_first = sorted(range(stops), key=lambda stop: -abs(stop - back_reach))

    def peers():
        for stop in far_first:
            for step in range(groups):
                if stop != back_reach or step != 0:
                    yield stop, stop - back_reach, moved(my_group, step, groups)

    barrier = pltpu.get_barrier_semaphore()
    for _, offset, group in peers():
        pl.semaphore_signal(
            barrier, inc=1,
            device_id={"acq": group, "rcv": moved(my_panel, offset, panels)},
            device_id_type=MESH,
        )

    small[0].wait()
    small[1].wait()
    small[2].wait()
    spectra = []
    for first in range(0, raw_slots, 2):
        blocks = list(range(first, min(first + 2, raw_slots)))
        for j in blocks:
            loads[j].wait()
        pair = jnp.concatenate([raw[j] for j in blocks], axis=1)
        both = jnp.dot(table[...], pair, preferred_element_type=F32)
        both = both.astype(BF16).astype(F32)
        for at in range(len(blocks)):
            spectra.append(both[:rows, at * width:(at + 1) * width])
    slot_of = [jnp.where(j < count[0], dest[j], -1) for j in range(raw_slots)]
    for owner in range(groups):
        total = jnp.zeros((rows, width), F32)
        for j in range(raw_slots):
            total = total + jnp.where(slot_of[j] == owner, 1.0, 0.0) * spectra[j]
        packed[owner] = total.astype(BF16)

    pl.semaphore_wait(barrier, groups * stops - 1)
    for stop, offset, group in peers():
        pltpu.make_async_remote_copy(
            src_ref=packed.at[group],
            dst_ref=received.at[stop, my_group],
            send_sem=send_sem,
            recv_sem=recv_sems.at[stop],
            device_id={"acq": group, "rcv": moved(my_panel, -offset, panels)},
            device_id_type=MESH,
        ).start()
    received[back_reach, my_group] = packed[my_group]

    for copy in small[3:]:
        copy.wait()
    slots[...] = jnp.zeros_like(slots)
    lane = lax.broadcasted_iota(jnp.int32, (width, width), 1)
    row = lax.broadcasted_iota(jnp.int32, (width, width), 0)
    for f in range(freq_count):
        for c in range(2):
            line = kern[f, c:c + 1, :].astype(F32)
            if c == 1:
                line = -line
            rolled = [
                pltpu.roll(
                    jnp.broadcast_to(line[:, at * width:(at + 1) * width], (width, width)),
                    0, 1, stride=1, stride_axis=0,
                )
                for at in range(stops + 1)
            ]
            for stop in range(stops):
                place = (2 * stop + c) * width
                operator[f, :, place:place + width] = jnp.where(
                    lane >= row, rolled[stop + 1], rolled[stop]
                ).astype(BF16)

    slot_at = lax.broadcasted_iota(jnp.int32, (groups * padded, shot_count), 0) // padded
    weights = weight[...].astype(F32)
    mixing = jnp.where(slot_at == stencil[0:1, :], weights[0:1, :], 0.0)
    mixing = mixing + jnp.where(slot_at == stencil[1:2, :], weights[1:2, :], 0.0)
    spread_rows = lax.broadcasted_iota(jnp.int32, (2 * shot_count, shot_count), 0)
    spread_cols = lax.broadcasted_iota(jnp.int32, (2 * shot_count, shot_count), 1)
    spread = jnp.where(spread_rows // 2 == spread_cols, 1.0, 0.0).astype(BF16)
    mixing = lax.dot_general(
        spread, mixing.astype(BF16), (((1,), (1,)), ((), ())), preferred_element_type=F32
    )
    part = lax.broadcasted_iota(jnp.int32, mixing.shape, 0) % 2
    component = lax.broadcasted_iota(jnp.int32, mixing.shape, 1) % padded
    mixers = []
    for f in range(freq_count):
        mixers.append(jnp.where(component == 2 * f + part, mixing, 0.0).astype(BF16))
        signed = jnp.where(part == 0, mixing, -mixing)
        mixers.append(jnp.where(component == 2 * f + 1 - part, signed, 0.0).astype(BF16))
    mixers = jnp.concatenate(mixers, axis=0)

    pairs = 2 * shot_count
    totals = [jnp.zeros((pairs, width), F32)] * freq_count
    for stop in reversed(far_first):
        arrived = received.at[stop]
        if stop == back_reach:
            arrived = received.at[stop, pl.ds(0, groups - 1)]
        pltpu.make_async_copy(arrived, arrived, recv_sems.at[stop]).wait()
        for group in range(groups):
            slots[stop, group * padded:group * padded + rows] = received[stop, group].astype(F32)
        regular = jnp.dot(
            mixers, slots[stop].astype(BF16), preferred_element_type=F32
        ).astype(BF16)
        for f in range(freq_count):
            at = 2 * f * pairs
            fields = jnp.concatenate(
                [regular[at:at + pairs], regular[at + pairs:at + 2 * pairs]], axis=1
            )
            totals[f] = totals[f] + lax.dot_general(
                fields, operator[f, :, 2 * stop * width:2 * (stop + 1) * width],
                (((1,), (1,)), ((), ())), preferred_element_type=F32,
            )
    for f in range(freq_count):
        out_ref[f] = totals[f].astype(BF16)

    for stop in range(stops):
        sent = packed
        if stop == back_reach:
            sent = packed.at[pl.ds(0, groups - 1)]
        pltpu.make_async_copy(sent, sent, send_sem).wait()


def shards(raw_blocks, raw_dest, raw_count, stencil, stencil_weight, kern):
    groups = lax.axis_size("acq")
    panels = lax.axis_size("rcv")
    stops = panels // 2
    raw_slots, sample_count, width = raw_blocks.shape
    freq_count = kern.shape[0]
    shot_count = stencil.shape[0]
    rows = 2 * freq_count
    padded = -(-rows // 8) * 8
    table = dft_table(freq_count, sample_count, -(-rows // 16) * 16)
    args = (table, raw_blocks, raw_dest, raw_count, stencil.T, stencil_weight.T, kern)
    out = pl.pallas_call(
        functools.partial(kernel, groups, panels, stops),
        out_shape=pltpu.VMEM((freq_count, 2 * shot_count, width), BF16),
        in_specs=[pl.BlockSpec(memory_space=pltpu.HBM)] * 7,
        out_specs=pl.BlockSpec(memory_space=pltpu.VMEM),
        scratch_shapes=[
            pltpu.VMEM(table.shape, BF16),
            pltpu.VMEM(raw_blocks.shape, BF16),
            pltpu.SMEM(raw_dest.shape, jnp.int32),
            pltpu.SMEM(raw_count.shape, jnp.int32),
            pltpu.VMEM((2, shot_count), jnp.int32),
            pltpu.VMEM((2, shot_count), BF16),
            pltpu.VMEM(kern.shape, BF16),
            pltpu.VMEM((groups, rows, width), BF16),
            pltpu.VMEM((stops, groups, rows, width), BF16),
            pltpu.VMEM((stops, groups * padded, width), F32),
            pltpu.VMEM((freq_count, width, 2 * stops * width), BF16),
            pltpu.SemaphoreType.DMA((raw_slots,)),
            pltpu.SemaphoreType.DMA((6,)),
            pltpu.SemaphoreType.DMA,
            pltpu.SemaphoreType.DMA((stops,)),
        ],
        compiler_params=pltpu.CompilerParams(
            collective_id=0, has_side_effects=True, vmem_limit_bytes=32 * 1024 * 1024
        ),
    )(*(pltpu.with_memory_space_constraint(arg, pltpu.HBM) if arg.size > 1 else arg for arg in args))
    return out.reshape(freq_count, shot_count, 1, 2, width)


def solution(mesh):
    return jax.shard_map(
        shards,
        mesh=mesh,
        in_specs=(P("acq", None, "rcv"), P("acq"), P("acq"), P("acq", None), P("acq", None), P()),
        out_specs=P(None, "acq", "rcv", None, None),
        check_vma=False,
    )
```

```python
import functools
import math

import jax
import jax.numpy as jnp
import numpy as np
from jax import lax
from jax.experimental import pallas as pl
from jax.experimental.pallas import tpu as pltpu
from jax.sharding import PartitionSpec as P

FLO = 32
MESH = pl.DeviceIdType.MESH
F32 = jnp.float32
BF16 = jnp.bfloat16


def dft_table(freq_count, sample_count, row_count):
    freqs = FLO + np.arange(freq_count, dtype=np.int32)
    samples = np.arange(sample_count, dtype=np.int32)
    angles = (freqs[:, None] * samples[None, :] % sample_count).astype(np.float32) * np.float32(
        2.0 * math.pi / sample_count
    )
    rows = np.stack([np.cos(angles), -np.sin(angles)], axis=1) / np.float32(math.sqrt(sample_count))
    table = np.zeros((row_count, sample_count), np.float32)
    table[: 2 * freq_count] = rows.reshape(2 * freq_count, sample_count)
    return jnp.asarray(table, BF16)


def kernel(
    groups, panels, stops,
    table_hbm, raw_hbm, dest_hbm, count_ref, stencil_hbm, weight_hbm, kern_hbm,
    out_ref,
    table, raw, dest, stencil, weight, kern, spectra, packed, received, operator,
    raw_sems, small_sems, shift_send_sems, shift_recv_sems, send_sem, recv_sem,
):
    raw_slots, _, width = raw.shape
    freq_count = kern.shape[0]
    rows = 2 * freq_count
    message_rows = packed.shape[1]
    shot_count = stencil.shape[1]
    back_reach = stops // 2 - 1
    my_group = lax.axis_index("acq")
    my_panel = lax.axis_index("rcv")

    small = [
        pltpu.make_async_copy(src, dst, small_sems.at[at])
        for at, (src, dst) in enumerate([
            (dest_hbm, dest), (stencil_hbm, stencil), (weight_hbm, weight), (table_hbm, table),
            (kern_hbm, kern),
        ])
    ]
    loads = [
        pltpu.make_async_copy(raw_hbm.at[j], raw.at[j], raw_sems.at[j]) for j in range(raw_slots)
    ]

    def moved(place, by, count):
        place = place + by
        if by < 0:
            return jnp.where(place < 0, place + count, place)
        return jnp.where(place >= count, place - count, place)

    def panel_at(offset):
        return {"acq": my_group, "rcv": moved(my_panel, offset, panels)}

    def group_at(step):
        return {"acq": moved(my_group, step, groups), "rcv": my_panel}

    far_stops = [stop for stop in range(stops) if stop != back_reach]
    barrier = pltpu.get_barrier_semaphore()
    for stop in far_stops:
        pl.semaphore_signal(
            barrier, inc=1, device_id=panel_at(stop - back_reach), device_id_type=MESH
        )
    for load in loads:
        load.start()
    for copy in small:
        copy.start()
    for step in range(1, groups):
        pl.semaphore_signal(barrier, inc=1, device_id=group_at(step), device_id_type=MESH)

    small[0].wait()
    select_shape = (groups * message_rows, stops * raw_slots * rows)
    select_row = lax.broadcasted_iota(jnp.int32, select_shape, 0)
    select_col = lax.broadcasted_iota(jnp.int32, select_shape, 1)
    owner_of = select_row // message_rows
    source = select_col // rows % raw_slots
    same_place = select_row % message_rows == (
        select_col // (raw_slots * rows) * rows + select_col % rows
    )
    target = jnp.full(select_shape, -1, jnp.int32)
    for j in range(raw_slots):
        target = jnp.where(source == j, jnp.where(j < count_ref[0], dest[j], -1), target)
    select = jnp.where(same_place & (owner_of == target), 1.0, 0.0).astype(BF16)

    small[1].wait()
    small[2].wait()
    tile = 8
    per_tile = tile // rows
    slot_at = lax.broadcasted_iota(jnp.int32, (groups * tile, shot_count), 0) // tile
    weights = weight[...].astype(F32)
    mixing = jnp.where(slot_at == stencil[0:1, :], weights[0:1, :], 0.0)
    mixing = mixing + jnp.where(slot_at == stencil[1:2, :], weights[1:2, :], 0.0)
    pairs = 2 * shot_count
    spread_rows = lax.broadcasted_iota(jnp.int32, (pairs, shot_count), 0)
    spread_cols = lax.broadcasted_iota(jnp.int32, (pairs, shot_count), 1)
    spread = jnp.where(spread_rows // 2 == spread_cols, 1.0, 0.0).astype(BF16)
    mixing = lax.dot_general(
        spread, mixing.astype(BF16), (((1,), (1,)), ((), ())), preferred_element_type=F32
    )
    part = lax.broadcasted_iota(jnp.int32, mixing.shape, 0) % 2
    signed = jnp.where(part == 0, mixing, -mixing)
    component = lax.broadcasted_iota(jnp.int32, mixing.shape, 1) % tile
    mixers = []
    for f in range(freq_count):
        for at in range(per_tile):
            first = at * rows + 2 * f
            mixers.append(jnp.where(component == first + part, mixing, 0.0).astype(BF16))
            mixers.append(jnp.where(component == first + 1 - part, signed, 0.0).astype(BF16))
    mixers = jnp.concatenate(mixers, axis=0)

    small[3].wait()
    pieces = []
    for first in range(0, raw_slots, 2):
        blocks = list(range(first, min(first + 2, raw_slots)))
        for j in blocks:
            loads[j].wait()
        pair = jnp.concatenate([raw[j] for j in blocks], axis=1)
        both = jnp.dot(table[...], pair, preferred_element_type=F32)
        for at in range(len(blocks)):
            pieces.append(both[:rows, at * width:(at + 1) * width])
    spectra[back_reach] = jnp.concatenate(pieces, axis=0).astype(BF16)

    pl.semaphore_wait(barrier, groups - 1 + stops - 1)
    shifts = [
        pltpu.make_async_remote_copy(
            src_ref=spectra.at[back_reach],
            dst_ref=spectra.at[stop],
            send_sem=shift_send_sems.at[stop],
            recv_sem=shift_recv_sems.at[stop],
            device_id=panel_at(back_reach - stop),
            device_id_type=MESH,
        )
        for stop in far_stops
    ]
    for shift in shifts:
        shift.start()

    lane = lax.broadcasted_iota(jnp.int32, (width, width), 1)
    row = lax.broadcasted_iota(jnp.int32, (width, width), 0)

    def fill_operator(f):
        for c in range(2):
            line = kern[f, c:c + 1, :].astype(F32)
            if c == 1:
                line = -line
            rolled = [
                pltpu.roll(
                    jnp.broadcast_to(line[:, at * width:(at + 1) * width], (width, width)),
                    0, 1, stride=1, stride_axis=0,
                )
                for at in range(stops + 1)
            ]
            for stop in range(stops):
                place = (2 * stop + c) * width
                operator[f, :, place:place + width] = jnp.where(
                    lane >= row, rolled[stop + 1], rolled[stop]
                ).astype(BF16)

    small[4].wait()
    for f in range(freq_count // 2):
        fill_operator(f)

    for shift in shifts:
        shift.wait_recv()
    gathered = jnp.dot(
        select, spectra[...].reshape(stops * raw_slots * rows, width), preferred_element_type=F32
    )
    packed[...] = gathered.reshape(groups, message_rows, width).astype(BF16)
    for step in range(1, groups):
        peer = group_at(step)
        pltpu.make_async_remote_copy(
            src_ref=packed.at[peer["acq"]],
            dst_ref=received.at[my_group],
            send_sem=send_sem,
            recv_sem=recv_sem,
            device_id=peer,
            device_id_type=MESH,
        ).start()
    received[my_group] = packed[my_group]
    for f in range(freq_count // 2, freq_count):
        fill_operator(f)

    arrived = received.at[pl.ds(0, groups - 1)]
    pltpu.make_async_copy(arrived, arrived, recv_sem).wait()
    slots = received[...].astype(F32)
    fields = [[] for _ in range(freq_count)]
    for first in range(0, stops, per_tile):
        start = first * rows
        part_slots = slots[:, start:start + tile].reshape(groups * tile, width).astype(BF16)
        regular = jnp.dot(mixers, part_slots, preferred_element_type=F32).astype(BF16)
        for f in range(freq_count):
            for at in range(2 * min(per_tile, stops - first)):
                place = (2 * f * per_tile + at) * pairs
                fields[f].append(regular[place:place + pairs])
    for f in range(freq_count):
        out_ref[f] = lax.dot_general(
            jnp.concatenate(fields[f], axis=1), operator[f], (((1,), (1,)), ((), ())),
            preferred_element_type=F32,
        ).astype(BF16)

    for shift in shifts:
        shift.wait_send()
    sent = packed.at[pl.ds(0, groups - 1)]
    pltpu.make_async_copy(sent, sent, send_sem).wait()


def shards(raw_blocks, raw_dest, raw_count, stencil, stencil_weight, kern):
    groups = lax.axis_size("acq")
    panels = lax.axis_size("rcv")
    stops = panels // 2
    raw_slots, sample_count, width = raw_blocks.shape
    freq_count = kern.shape[0]
    shot_count = stencil.shape[0]
    rows = 2 * freq_count
    message_rows = -(-stops * rows // 8) * 8
    table = dft_table(freq_count, sample_count, -(-rows // 16) * 16)
    args = (table, raw_blocks, raw_dest, raw_count, stencil.T, stencil_weight.T, kern)
    out = pl.pallas_call(
        functools.partial(kernel, groups, panels, stops),
        out_shape=pltpu.VMEM((freq_count, 2 * shot_count, width), BF16),
        in_specs=[
            pl.BlockSpec(memory_space=pltpu.SMEM if arg is raw_count else pltpu.HBM)
            for arg in args
        ],
        out_specs=pl.BlockSpec(memory_space=pltpu.VMEM),
        scratch_shapes=[
            pltpu.VMEM(table.shape, BF16),
            pltpu.VMEM(raw_blocks.shape, BF16),
            pltpu.SMEM(raw_dest.shape, jnp.int32),
            pltpu.VMEM((2, shot_count), jnp.int32),
            pltpu.VMEM((2, shot_count), BF16),
            pltpu.VMEM(kern.shape, BF16),
            pltpu.VMEM((stops, raw_slots * rows, width), BF16),
            pltpu.VMEM((groups, message_rows, width), BF16),
            pltpu.VMEM((groups, message_rows, width), BF16),
            pltpu.VMEM((freq_count, width, 2 * stops * width), BF16),
            pltpu.SemaphoreType.DMA((raw_slots,)),
            pltpu.SemaphoreType.DMA((5,)),
            pltpu.SemaphoreType.DMA((stops,)),
            pltpu.SemaphoreType.DMA((stops,)),
            pltpu.SemaphoreType.DMA,
            pltpu.SemaphoreType.DMA,
        ],
        compiler_params=pltpu.CompilerParams(
            collective_id=0, has_side_effects=True, vmem_limit_bytes=32 * 1024 * 1024
        ),
    )(*(
        arg if arg is raw_count else pltpu.with_memory_space_constraint(arg, pltpu.HBM)
        for arg in args
    ))
    return out.reshape(freq_count, shot_count, 1, 2, width)


def solution(mesh):
    return jax.shard_map(
        shards,
        mesh=mesh,
        in_specs=(P("acq", None, "rcv"), P("acq"), P("acq"), P("acq", None), P("acq", None), P()),
        out_specs=P(None, "acq", "rcv", None, None),
        check_vma=False,
    )
```

```python
import functools
import math

import jax
import jax.numpy as jnp
import numpy as np
from jax import lax
from jax.experimental import pallas as pl
from jax.experimental.pallas import tpu as pltpu
from jax.sharding import PartitionSpec as P

FLO = 32
MESH = pl.DeviceIdType.MESH
F32 = jnp.float32
BF16 = jnp.bfloat16


def dft_table(freq_count, sample_count, row_count):
    freqs = FLO + np.arange(freq_count, dtype=np.int32)
    samples = np.arange(sample_count, dtype=np.int32)
    angles = (freqs[:, None] * samples[None, :] % sample_count).astype(np.float32) * np.float32(
        2.0 * math.pi / sample_count
    )
    rows = np.stack([np.cos(angles), -np.sin(angles)], axis=1) / np.float32(math.sqrt(sample_count))
    table = np.zeros((row_count, sample_count), np.float32)
    table[: 2 * freq_count] = rows.reshape(2 * freq_count, sample_count)
    return jnp.asarray(table, BF16)


def split(index, size):
    if size & (size - 1):
        return index // size, index % size
    return index >> (size.bit_length() - 1), index & (size - 1)


def kernel(
    groups, panels, stops,
    table_hbm, raw_hbm, dest_hbm, count_ref, stencil_hbm, weight_hbm, kern_hbm,
    out_ref,
    table, raw, dest, stencil, weight, kern, spectra, packed, received, operator,
    raw_sems, small_sems, shift_send_sems, shift_recv_sems, send_sem, recv_sem,
):
    raw_slots, sample_count, width = raw.shape
    depth = sample_count // raw_sems.shape[1]
    freq_count = kern.shape[0]
    rows = 2 * freq_count
    message_rows = packed.shape[1]
    shot_count = stencil.shape[1]
    back_reach = stops // 2 - 1
    my_group = lax.axis_index("acq")
    my_panel = lax.axis_index("rcv")

    small = [
        pltpu.make_async_copy(src, dst, small_sems.at[at])
        for at, (src, dst) in enumerate([
            (dest_hbm, dest), (stencil_hbm, stencil), (weight_hbm, weight), (table_hbm, table),
            (kern_hbm, kern),
        ])
    ]
    loads = [
        [
            pltpu.make_async_copy(
                raw_hbm.at[j, pl.ds(first, depth)], raw.at[j, pl.ds(first, depth)],
                raw_sems.at[j, at],
            )
            for at, first in enumerate(range(0, sample_count, depth))
        ]
        for j in range(raw_slots)
    ]

    def moved(place, by, count):
        place = place + by
        if by < 0:
            return jnp.where(place < 0, place + count, place)
        return jnp.where(place >= count, place - count, place)

    def panel_at(offset):
        return {"acq": my_group, "rcv": moved(my_panel, offset, panels)}

    def group_at(step):
        return {"acq": moved(my_group, step, groups), "rcv": my_panel}

    far_stops = [stop for stop in range(stops) if stop != back_reach]
    barrier = pltpu.get_barrier_semaphore()
    for stop in far_stops:
        pl.semaphore_signal(
            barrier, inc=1, device_id=panel_at(stop - back_reach), device_id_type=MESH
        )
    for block in loads:
        for load in block:
            load.start()
    for copy in small:
        copy.start()
    for step in range(1, groups):
        pl.semaphore_signal(barrier, inc=1, device_id=group_at(step), device_id_type=MESH)

    small[0].wait()
    select_shape = (groups * message_rows, stops * raw_slots * rows)
    select_row = lax.broadcasted_iota(jnp.int32, select_shape, 0)
    select_col = lax.broadcasted_iota(jnp.int32, select_shape, 1)
    owner_of, message_row = split(select_row, message_rows)
    block_of, source_row = split(select_col, rows)
    source_stop, source = split(block_of, raw_slots)
    same_place = message_row == source_stop * rows + source_row
    target = jnp.full(select_shape, -1, jnp.int32)
    for j in range(raw_slots):
        target = jnp.where(source == j, jnp.where(j < count_ref[0], dest[j], -1), target)
    select = jnp.where(same_place & (owner_of == target), 1.0, 0.0).astype(BF16)

    small[3].wait()
    pieces = []
    for first in range(0, raw_slots, 2):
        blocks = list(range(first, min(first + 2, raw_slots)))
        both = None
        for at in range(sample_count // depth):
            for j in blocks:
                loads[j][at].wait()
            span = slice(at * depth, (at + 1) * depth)
            term = jnp.dot(
                table[:, span], jnp.concatenate([raw[j, span] for j in blocks], axis=1),
                preferred_element_type=F32,
            )
            both = term if both is None else both + term
        for at in range(len(blocks)):
            pieces.append(both[:rows, at * width:(at + 1) * width])
    spectra[back_reach] = jnp.concatenate(pieces, axis=0).astype(BF16)

    pl.semaphore_wait(barrier, groups - 1 + stops - 1)
    shifts = [
        pltpu.make_async_remote_copy(
            src_ref=spectra.at[back_reach],
            dst_ref=spectra.at[stop],
            send_sem=shift_send_sems.at[stop],
            recv_sem=shift_recv_sems.at[stop],
            device_id=panel_at(back_reach - stop),
            device_id_type=MESH,
        )
        for stop in far_stops
    ]
    for shift in shifts:
        shift.start()

    small[1].wait()
    small[2].wait()
    tile = 8
    per_tile = tile // rows
    slot_at, _ = split(lax.broadcasted_iota(jnp.int32, (groups * tile, shot_count), 0), tile)
    weights = weight[...].astype(F32)
    mixing = jnp.where(slot_at == stencil[0:1, :], weights[0:1, :], 0.0)
    mixing = mixing + jnp.where(slot_at == stencil[1:2, :], weights[1:2, :], 0.0)
    pairs = 2 * shot_count
    spread_rows = lax.broadcasted_iota(jnp.int32, (pairs, shot_count), 0)
    spread_cols = lax.broadcasted_iota(jnp.int32, (pairs, shot_count), 1)
    spread = jnp.where(split(spread_rows, 2)[0] == spread_cols, 1.0, 0.0).astype(BF16)
    mixing = lax.dot_general(
        spread, mixing.astype(BF16), (((1,), (1,)), ((), ())), preferred_element_type=F32
    )
    _, part = split(lax.broadcasted_iota(jnp.int32, mixing.shape, 0), 2)
    signed = jnp.where(part == 0, mixing, -mixing)
    _, component = split(lax.broadcasted_iota(jnp.int32, mixing.shape, 1), tile)
    mixers = []
    for f in range(freq_count):
        for at in range(per_tile):
            first = at * rows + 2 * f
            mixers.append(jnp.where(component == first + part, mixing, 0.0).astype(BF16))
            mixers.append(jnp.where(component == first + 1 - part, signed, 0.0).astype(BF16))
    mixers = jnp.concatenate(mixers, axis=0)

    small[4].wait()
    lane = lax.broadcasted_iota(jnp.int32, (width, width), 1)
    row = lax.broadcasted_iota(jnp.int32, (width, width), 0)
    flip = jnp.where(lane + row == width - 1, 1.0, 0.0).astype(BF16)
    lines = jnp.concatenate([kern[f].astype(F32) for f in range(freq_count)], axis=0).astype(BF16)
    flipped = [
        jnp.dot(lines[:, at * width:(at + 1) * width], flip, preferred_element_type=F32)
        for at in range(stops + 1)
    ]
    for f in range(freq_count):
        for c in range(2):
            line = 2 * f + c
            rolled = []
            for at in range(stops + 1):
                piece = flipped[at][line:line + 1]
                piece = -piece if c == 1 else piece
                rolled.append(pltpu.roll(
                    jnp.broadcast_to(piece, (width, width)), 1, 1, stride=1, stride_axis=0
                ))
            for stop in range(stops):
                place = (2 * stop + c) * width
                operator[f, place:place + width] = jnp.where(
                    row >= lane, rolled[stop + 1], rolled[stop]
                ).astype(BF16)

    for shift in shifts:
        shift.wait_recv()
    gathered = jnp.dot(
        select, spectra[...].reshape(stops * raw_slots * rows, width), preferred_element_type=F32
    )
    packed[...] = gathered.reshape(groups, message_rows, width).astype(BF16)
    for step in range(1, groups):
        peer = group_at(step)
        pltpu.make_async_remote_copy(
            src_ref=packed.at[peer["acq"]],
            dst_ref=received.at[my_group],
            send_sem=send_sem,
            recv_sem=recv_sem,
            device_id=peer,
            device_id_type=MESH,
        ).start()
    received[my_group] = packed[my_group]

    arrived = received.at[pl.ds(0, groups - 1)]
    pltpu.make_async_copy(arrived, arrived, recv_sem).wait()
    slots = received[...].astype(F32)
    fields = [[] for _ in range(freq_count)]
    for first in range(0, stops, per_tile):
        start = first * rows
        part_slots = slots[:, start:start + tile].reshape(groups * tile, width).astype(BF16)
        regular = jnp.dot(mixers, part_slots, preferred_element_type=F32).astype(BF16)
        for f in range(freq_count):
            for at in range(2 * min(per_tile, stops - first)):
                place = (2 * f * per_tile + at) * pairs
                fields[f].append(regular[place:place + pairs])
    for f in range(freq_count):
        out_ref[f] = jnp.dot(
            jnp.concatenate(fields[f], axis=1), operator[f], preferred_element_type=F32
        ).astype(BF16)

    for shift in shifts:
        shift.wait_send()
    sent = packed.at[pl.ds(0, groups - 1)]
    pltpu.make_async_copy(sent, sent, send_sem).wait()


def shards(raw_blocks, raw_dest, raw_count, stencil, stencil_weight, kern):
    groups = lax.axis_size("acq")
    panels = lax.axis_size("rcv")
    stops = panels // 2
    raw_slots, sample_count, width = raw_blocks.shape
    freq_count = kern.shape[0]
    shot_count = stencil.shape[0]
    rows = 2 * freq_count
    message_rows = -(-stops * rows // 8) * 8
    table = dft_table(freq_count, sample_count, -(-rows // 16) * 16)
    args = (table, raw_blocks, raw_dest, raw_count, stencil.T, stencil_weight.T, kern)
    out = pl.pallas_call(
        functools.partial(kernel, groups, panels, stops),
        out_shape=pltpu.VMEM((freq_count, 2 * shot_count, width), BF16),
        in_specs=[
            pl.BlockSpec(memory_space=pltpu.SMEM if arg is raw_count else pltpu.HBM)
            for arg in args
        ],
        out_specs=pl.BlockSpec(memory_space=pltpu.VMEM),
        scratch_shapes=[
            pltpu.VMEM(table.shape, BF16),
            pltpu.VMEM(raw_blocks.shape, BF16),
            pltpu.SMEM(raw_dest.shape, jnp.int32),
            pltpu.VMEM((2, shot_count), jnp.int32),
            pltpu.VMEM((2, shot_count), BF16),
            pltpu.VMEM(kern.shape, BF16),
            pltpu.VMEM((stops, raw_slots * rows, width), BF16),
            pltpu.VMEM((groups, message_rows, width), BF16),
            pltpu.VMEM((groups, message_rows, width), BF16),
            pltpu.VMEM((freq_count, 2 * stops * width, width), BF16),
            pltpu.SemaphoreType.DMA((raw_slots, 2)),
            pltpu.SemaphoreType.DMA((5,)),
            pltpu.SemaphoreType.DMA((stops,)),
            pltpu.SemaphoreType.DMA((stops,)),
            pltpu.SemaphoreType.DMA,
            pltpu.SemaphoreType.DMA,
        ],
        compiler_params=pltpu.CompilerParams(
            collective_id=0, has_side_effects=True, vmem_limit_bytes=32 * 1024 * 1024
        ),
    )(*(
        arg if arg is raw_count else pltpu.with_memory_space_constraint(arg, pltpu.HBM)
        for arg in args
    ))
    return out.reshape(freq_count, shot_count, 1, 2, width)


def solution(mesh):
    return jax.shard_map(
        shards,
        mesh=mesh,
        in_specs=(P("acq", None, "rcv"), P("acq"), P("acq"), P("acq", None), P("acq", None), P()),
        out_specs=P(None, "acq", "rcv", None, None),
        check_vma=False,
    )
```

```python
import functools
import math

import jax
import jax.numpy as jnp
import numpy as np
from jax import lax
from jax.experimental import pallas as pl
from jax.experimental.pallas import tpu as pltpu
from jax.sharding import PartitionSpec as P

FLO = 32
MESH = pl.DeviceIdType.MESH
F32 = jnp.float32
BF16 = jnp.bfloat16


def dft_table(freq_count, sample_count, row_count):
    freqs = FLO + np.arange(freq_count, dtype=np.int32)
    samples = np.arange(sample_count, dtype=np.int32)
    angles = (freqs[:, None] * samples[None, :] % sample_count).astype(np.float32) * np.float32(
        2.0 * math.pi / sample_count
    )
    rows = np.stack([np.cos(angles), -np.sin(angles)], axis=1) / np.float32(math.sqrt(sample_count))
    table = np.zeros((row_count, sample_count), np.float32)
    table[: 2 * freq_count] = rows.reshape(2 * freq_count, sample_count)
    return jnp.asarray(table, BF16)


def split(index, size):
    if size & (size - 1):
        return index // size, index % size
    return index >> (size.bit_length() - 1), index & (size - 1)


def kernel(
    groups, panels, stops,
    table_hbm, raw_hbm, dest_hbm, count_ref, stencil_hbm, weight_hbm, kern_hbm,
    out_ref,
    table, raw, dest, stencil, weight, kern, packed, received, slots, operator,
    raw_sems, small_sems, send_sem, recv_sems,
):
    raw_slots, sample_count, width = raw.shape
    depth = sample_count // raw_sems.shape[1]
    freq_count = kern.shape[0]
    rows = 2 * freq_count
    tile = -(-rows // 8) * 8
    shot_count = stencil.shape[1]
    back_reach = stops // 2 - 1
    my_group = lax.axis_index("acq")
    my_panel = lax.axis_index("rcv")

    small = [
        pltpu.make_async_copy(src, dst, small_sems.at[at])
        for at, (src, dst) in enumerate([
            (dest_hbm, dest), (stencil_hbm, stencil), (weight_hbm, weight), (table_hbm, table),
            (kern_hbm, kern),
        ])
    ]
    loads = [
        [
            pltpu.make_async_copy(
                raw_hbm.at[j, pl.ds(first, depth)], raw.at[j, pl.ds(first, depth)],
                raw_sems.at[j, at],
            )
            for at, first in enumerate(range(0, sample_count, depth))
        ]
        for j in range(raw_slots)
    ]

    def moved(place, by, count):
        place = place + by
        if by < 0:
            return jnp.where(place < 0, place + count, place)
        return jnp.where(place >= count, place - count, place)

    far_first = sorted(range(stops), key=lambda stop: -abs(stop - back_reach))

    def peers(sign):
        for stop in far_first:
            panel = moved(my_panel, sign * (stop - back_reach), panels)
            for step in range(groups):
                if stop != back_reach or step != 0:
                    group = moved(my_group, step, groups)
                    yield stop, group, {"acq": group, "rcv": panel}

    barrier = pltpu.get_barrier_semaphore()
    for _, _, peer in peers(1):
        pl.semaphore_signal(barrier, inc=1, device_id=peer, device_id_type=MESH)
    for block in loads:
        for load in block:
            load.start()
    for copy in small:
        copy.start()
    slots[...] = jnp.zeros_like(slots)
    small[0].wait()
    select_shape = (groups * tile, raw_slots * rows)
    owner_of, place_row = split(lax.broadcasted_iota(jnp.int32, select_shape, 0), tile)
    source, source_row = split(lax.broadcasted_iota(jnp.int32, select_shape, 1), rows)
    same_place = place_row == source_row
    target = jnp.full(select_shape, -1, jnp.int32)
    for j in range(raw_slots):
        target = jnp.where(source == j, jnp.where(j < count_ref[0], dest[j], -1), target)
    select = jnp.where(same_place & (owner_of == target), 1.0, 0.0).astype(BF16)

    small[1].wait()
    small[2].wait()
    slot_at, _ = split(lax.broadcasted_iota(jnp.int32, (groups * tile, shot_count), 0), tile)
    weights = weight[...].astype(F32)
    mixing = jnp.where(slot_at == stencil[0:1, :], weights[0:1, :], 0.0)
    mixing = mixing + jnp.where(slot_at == stencil[1:2, :], weights[1:2, :], 0.0)
    pairs = 2 * shot_count
    spread_rows = lax.broadcasted_iota(jnp.int32, (pairs, shot_count), 0)
    spread_cols = lax.broadcasted_iota(jnp.int32, (pairs, shot_count), 1)
    spread = jnp.where(split(spread_rows, 2)[0] == spread_cols, 1.0, 0.0).astype(BF16)
    mixing = lax.dot_general(
        spread, mixing.astype(BF16), (((1,), (1,)), ((), ())), preferred_element_type=F32
    )
    _, part = split(lax.broadcasted_iota(jnp.int32, mixing.shape, 0), 2)
    signed = jnp.where(part == 0, mixing, -mixing)
    _, component = split(lax.broadcasted_iota(jnp.int32, mixing.shape, 1), tile)
    mixers = []
    for f in range(freq_count):
        mixers.append(jnp.where(component == 2 * f + part, mixing, 0.0).astype(BF16))
        mixers.append(jnp.where(component == 2 * f + 1 - part, signed, 0.0).astype(BF16))
    mixers = jnp.concatenate(mixers, axis=0)

    small[4].wait()
    lane = lax.broadcasted_iota(jnp.int32, (width, width), 1)
    row = lax.broadcasted_iota(jnp.int32, (width, width), 0)
    flip = jnp.where(lane + row == width - 1, 1.0, 0.0).astype(BF16)
    lines = jnp.concatenate([kern[f].astype(F32) for f in range(freq_count)], axis=0).astype(BF16)
    flipped = [
        jnp.dot(lines[:, at * width:(at + 1) * width], flip, preferred_element_type=F32)
        for at in range(stops + 1)
    ]
    for f in range(freq_count):
        for c in range(2):
            line = 2 * f + c
            rolled = []
            for at in range(stops + 1):
                piece = flipped[at][line:line + 1]
                piece = -piece if c == 1 else piece
                rolled.append(pltpu.roll(
                    jnp.broadcast_to(piece, (width, width)), 1, 1, stride=1, stride_axis=0
                ))
            for stop in range(stops):
                place = (2 * stop + c) * width
                operator[f, place:place + width] = jnp.where(
                    row >= lane, rolled[stop + 1], rolled[stop]
                ).astype(BF16)

    small[3].wait()
    pieces = []
    for first in range(0, raw_slots, 2):
        blocks = list(range(first, min(first + 2, raw_slots)))
        both = None
        for at in range(sample_count // depth):
            for j in blocks:
                loads[j][at].wait()
            span = slice(at * depth, (at + 1) * depth)
            term = jnp.dot(
                table[:, span], jnp.concatenate([raw[j, span] for j in blocks], axis=1),
                preferred_element_type=F32,
            )
            both = term if both is None else both + term
        for at in range(len(blocks)):
            pieces.append(both[:rows, at * width:(at + 1) * width])
    spectra = jnp.concatenate(pieces, axis=0).astype(BF16)
    gathered = jnp.dot(select, spectra, preferred_element_type=F32)
    for owner in range(groups):
        packed[owner] = gathered[owner * tile:owner * tile + rows].astype(BF16)

    pl.semaphore_wait(barrier, groups * stops - 1)
    for stop, group, peer in peers(-1):
        pltpu.make_async_remote_copy(
            src_ref=packed.at[group],
            dst_ref=received.at[stop, my_group],
            send_sem=send_sem,
            recv_sem=recv_sems.at[stop],
            device_id=peer,
            device_id_type=MESH,
        ).start()
    received[back_reach, my_group] = packed[my_group]

    totals = [jnp.zeros((pairs, width), F32)] * freq_count
    for stop in reversed(far_first):
        arrived = received.at[stop]
        if stop == back_reach:
            arrived = received.at[stop, pl.ds(0, groups - 1)]
        pltpu.make_async_copy(arrived, arrived, recv_sems.at[stop]).wait()
        for group in range(groups):
            slots[stop, group * tile:group * tile + rows] = received[stop, group].astype(F32)
        regular = jnp.dot(
            mixers, slots[stop].astype(BF16), preferred_element_type=F32
        ).astype(BF16)
        for f in range(freq_count):
            at = 2 * f * pairs
            fields = jnp.concatenate(
                [regular[at:at + pairs], regular[at + pairs:at + 2 * pairs]], axis=1
            )
            totals[f] = totals[f] + jnp.dot(
                fields, operator[f, 2 * stop * width:2 * (stop + 1) * width],
                preferred_element_type=F32,
            )
    for f in range(freq_count):
        out_ref[f] = totals[f].astype(BF16)

    for stop in range(stops):
        sent = packed
        if stop == back_reach:
            sent = packed.at[pl.ds(0, groups - 1)]
        pltpu.make_async_copy(sent, sent, send_sem).wait()


def shards(raw_blocks, raw_dest, raw_count, stencil, stencil_weight, kern):
    groups = lax.axis_size("acq")
    panels = lax.axis_size("rcv")
    stops = panels // 2
    raw_slots, sample_count, width = raw_blocks.shape
    freq_count = kern.shape[0]
    shot_count = stencil.shape[0]
    rows = 2 * freq_count
    tile = -(-rows // 8) * 8
    table = dft_table(freq_count, sample_count, -(-rows // 16) * 16)
    args = (table, raw_blocks, raw_dest, raw_count, stencil.T, stencil_weight.T, kern)
    out = pl.pallas_call(
        functools.partial(kernel, groups, panels, stops),
        out_shape=pltpu.VMEM((freq_count, 2 * shot_count, width), BF16),
        in_specs=[
            pl.BlockSpec(memory_space=pltpu.SMEM if arg is raw_count else pltpu.HBM)
            for arg in args
        ],
        out_specs=pl.BlockSpec(memory_space=pltpu.VMEM),
        scratch_shapes=[
            pltpu.VMEM(table.shape, BF16),
            pltpu.VMEM(raw_blocks.shape, BF16),
            pltpu.SMEM(raw_dest.shape, jnp.int32),
            pltpu.VMEM((2, shot_count), jnp.int32),
            pltpu.VMEM((2, shot_count), BF16),
            pltpu.VMEM(kern.shape, BF16),
            pltpu.VMEM((groups, rows, width), BF16),
            pltpu.VMEM((stops, groups, rows, width), BF16),
            pltpu.VMEM((stops, groups * tile, width), F32),
            pltpu.VMEM((freq_count, 2 * stops * width, width), BF16),
            pltpu.SemaphoreType.DMA((raw_slots, 2)),
            pltpu.SemaphoreType.DMA((5,)),
            pltpu.SemaphoreType.DMA,
            pltpu.SemaphoreType.DMA((stops,)),
        ],
        compiler_params=pltpu.CompilerParams(
            collective_id=0, has_side_effects=True, vmem_limit_bytes=32 * 1024 * 1024
        ),
    )(*(
        arg if arg is raw_count else pltpu.with_memory_space_constraint(arg, pltpu.HBM)
        for arg in args
    ))
    return out.reshape(freq_count, shot_count, 1, 2, width)


def solution(mesh):
    return jax.shard_map(
        shards,
        mesh=mesh,
        in_specs=(P("acq", None, "rcv"), P("acq"), P("acq"), P("acq", None), P("acq", None), P()),
        out_specs=P(None, "acq", "rcv", None, None),
        check_vma=False,
    )
```

```python
import functools
import math

import jax
import jax.numpy as jnp
import numpy as np
from jax import lax
from jax.experimental import pallas as pl
from jax.experimental.pallas import tpu as pltpu
from jax.sharding import PartitionSpec as P

FLO = 32
MESH = pl.DeviceIdType.MESH
F32 = jnp.float32
BF16 = jnp.bfloat16


def dft_table(freq_count, sample_count, row_count):
    freqs = FLO + np.arange(freq_count, dtype=np.int32)
    samples = np.arange(sample_count, dtype=np.int32)
    angles = (freqs[:, None] * samples[None, :] % sample_count).astype(np.float32) * np.float32(
        2.0 * math.pi / sample_count
    )
    rows = np.stack([np.cos(angles), -np.sin(angles)], axis=1) / np.float32(math.sqrt(sample_count))
    table = np.zeros((row_count, sample_count), np.float32)
    table[: 2 * freq_count] = rows.reshape(2 * freq_count, sample_count)
    return jnp.asarray(table, BF16)


def split(index, size):
    if size & (size - 1):
        return index // size, index % size
    return index >> (size.bit_length() - 1), index & (size - 1)


def kernel(
    groups, panels, stops,
    table_hbm, raw_hbm, dest_hbm, count_ref, stencil_hbm, weight_hbm, kern_hbm,
    out_ref,
    table, raw, dest, stencil, weight, kern, packed, received, relay, slots, mixers, operator,
    raw_sems, small_sems, send_sem, recv_sems, relay_sems,
):
    raw_slots, sample_count, width = raw.shape
    depth = sample_count // raw_sems.shape[1]
    freq_count = kern.shape[0]
    rows = 2 * freq_count
    tile = -(-rows // 8) * 8
    shot_count = stencil.shape[1]
    pairs = 2 * shot_count
    back_reach = stops // 2 - 1
    my_group = lax.axis_index("acq")
    my_panel = lax.axis_index("rcv")

    small = [
        pltpu.make_async_copy(src, dst, small_sems.at[at])
        for at, (src, dst) in enumerate([
            (dest_hbm, dest), (stencil_hbm, stencil), (weight_hbm, weight), (table_hbm, table),
            (kern_hbm, kern),
        ])
    ]
    loads = [
        [
            pltpu.make_async_copy(
                raw_hbm.at[j, pl.ds(first, depth)], raw.at[j, pl.ds(first, depth)],
                raw_sems.at[j, at],
            )
            for at, first in enumerate(range(0, sample_count, depth))
        ]
        for j in range(raw_slots)
    ]

    def moved(place, by, count):
        place = place + by
        if by < 0:
            return jnp.where(place < 0, place + count, place)
        return jnp.where(place >= count, place - count, place)

    far_first = sorted(range(stops), key=lambda stop: -abs(stop - back_reach))

    def peers(sign):
        for stop in far_first:
            panel = moved(my_panel, sign * (stop - back_reach), panels)
            for step in range(groups):
                if stop != back_reach or step != 0:
                    group = moved(my_group, step, groups)
                    yield stop, group, {"acq": group, "rcv": panel}

    relayed = stops == 2 and panels >= 4
    last = panels - 1
    relay_panel = panels - 2
    barrier = pltpu.get_barrier_semaphore()

    def greet(group, panel):
        pl.semaphore_signal(
            barrier, inc=1, device_id={"acq": group, "rcv": panel}, device_id_type=MESH
        )

    if relayed:
        @pl.when(my_panel == relay_panel)
        def _():
            greet(my_group, 0)

        sender_panel = jnp.where(my_panel == last, relay_panel, my_panel + 1)
        for step in range(groups):
            greet(moved(my_group, step, groups), sender_panel)
        for step in range(1, groups):
            greet(moved(my_group, step, groups), my_panel)
    else:
        for _, group, peer in peers(1):
            greet(group, peer["rcv"])
    for block in loads:
        for load in block:
            load.start()
    for copy in small:
        copy.start()
    slots[...] = jnp.zeros_like(slots)
    small[0].wait()
    select_shape = (groups * tile, raw_slots * rows)
    owner_of, place_row = split(lax.broadcasted_iota(jnp.int32, select_shape, 0), tile)
    source, source_row = split(lax.broadcasted_iota(jnp.int32, select_shape, 1), rows)
    same_place = place_row == source_row
    target = jnp.full(select_shape, -1, jnp.int32)
    for j in range(raw_slots):
        target = jnp.where(source == j, jnp.where(j < count_ref[0], dest[j], -1), target)
    select = jnp.where(same_place & (owner_of == target), 1.0, 0.0).astype(BF16)

    def prepare():
        small[1].wait()
        small[2].wait()
        slot_at, _ = split(lax.broadcasted_iota(jnp.int32, (groups * tile, shot_count), 0), tile)
        weights = weight[...].astype(F32)
        mixing = jnp.where(slot_at == stencil[0:1, :], weights[0:1, :], 0.0)
        mixing = mixing + jnp.where(slot_at == stencil[1:2, :], weights[1:2, :], 0.0)
        spread_rows = lax.broadcasted_iota(jnp.int32, (pairs, shot_count), 0)
        spread_cols = lax.broadcasted_iota(jnp.int32, (pairs, shot_count), 1)
        spread = jnp.where(split(spread_rows, 2)[0] == spread_cols, 1.0, 0.0).astype(BF16)
        mixing = lax.dot_general(
            spread, mixing.astype(BF16), (((1,), (1,)), ((), ())), preferred_element_type=F32
        )
        _, part = split(lax.broadcasted_iota(jnp.int32, mixing.shape, 0), 2)
        signed = jnp.where(part == 0, mixing, -mixing)
        _, component = split(lax.broadcasted_iota(jnp.int32, mixing.shape, 1), tile)
        for f in range(freq_count):
            mixers[2 * f * pairs:(2 * f + 1) * pairs] = (
                jnp.where(component == 2 * f + part, mixing, 0.0).astype(BF16)
            )
            mixers[(2 * f + 1) * pairs:(2 * f + 2) * pairs] = (
                jnp.where(component == 2 * f + 1 - part, signed, 0.0).astype(BF16)
            )

        small[4].wait()
        lane = lax.broadcasted_iota(jnp.int32, (width, width), 1)
        row = lax.broadcasted_iota(jnp.int32, (width, width), 0)
        flip = jnp.where(lane + row == width - 1, 1.0, 0.0).astype(BF16)
        lines = jnp.concatenate([kern[f].astype(F32) for f in range(freq_count)], axis=0).astype(BF16)
        flipped = [
            jnp.dot(lines[:, at * width:(at + 1) * width], flip, preferred_element_type=F32)
            for at in range(stops + 1)
        ]
        for f in range(freq_count):
            for c in range(2):
                line = 2 * f + c
                rolled = []
                for at in range(stops + 1):
                    piece = flipped[at][line:line + 1]
                    piece = -piece if c == 1 else piece
                    rolled.append(pltpu.roll(
                        jnp.broadcast_to(piece, (width, width)), 1, 1, stride=1, stride_axis=0
                    ))
                for stop in range(stops):
                    place = (2 * stop + c) * width
                    operator[f, place:place + width] = jnp.where(
                        row >= lane, rolled[stop + 1], rolled[stop]
                    ).astype(BF16)

    if relayed:
        waits_long = (my_panel == 0) | (my_panel == relay_panel)
        pl.when(waits_long)(prepare)
    small[3].wait()
    pieces = []
    for first in range(0, raw_slots, 2):
        blocks = list(range(first, min(first + 2, raw_slots)))
        both = None
        for at in range(sample_count // depth):
            for j in blocks:
                loads[j][at].wait()
            span = slice(at * depth, (at + 1) * depth)
            term = jnp.dot(
                table[:, span], jnp.concatenate([raw[j, span] for j in blocks], axis=1),
                preferred_element_type=F32,
            )
            both = term if both is None else both + term
        for at in range(len(blocks)):
            pieces.append(both[:rows, at * width:(at + 1) * width])
    spectra = jnp.concatenate(pieces, axis=0).astype(BF16)
    gathered = jnp.dot(select, spectra, preferred_element_type=F32)
    for owner in range(groups):
        packed[owner] = gathered[owner * tile:owner * tile + rows].astype(BF16)

    def send(src, dst, send_to, recv_to, group, panel):
        pltpu.make_async_remote_copy(
            src_ref=src, dst_ref=dst, send_sem=send_to, recv_sem=recv_to,
            device_id={"acq": group, "rcv": panel}, device_id_type=MESH,
        ).start()

    if relayed:
        @pl.when(my_panel == 0)
        def _():
            pl.semaphore_wait(barrier, groups)
            send(packed, relay, send_sem, relay_sems.at[0], my_group, relay_panel)

        @pl.when(my_panel == relay_panel)
        def _():
            pl.semaphore_wait(barrier, 3 * groups - 1)

        @pl.when((my_panel == last) | ((my_panel > 0) & (my_panel < relay_panel)))
        def _():
            pl.semaphore_wait(barrier, 2 * groups - 1)

        @pl.when(my_panel > 0)
        def _():
            for step in range(groups):
                group = moved(my_group, step, groups)
                send(
                    packed.at[group], received.at[1, my_group], send_sem, recv_sems.at[1],
                    group, my_panel - 1,
                )

        for step in range(1, groups):
            group = moved(my_group, step, groups)
            send(
                packed.at[group], received.at[0, my_group], send_sem, recv_sems.at[0],
                group, my_panel,
            )

        @pl.when(my_panel == relay_panel)
        def _():
            pltpu.make_async_copy(relay, relay, relay_sems.at[0]).wait()
            for step in range(groups):
                group = moved(my_group, step, groups)
                send(
                    relay.at[group], received.at[1, my_group], relay_sems.at[1], recv_sems.at[1],
                    group, last,
                )

        received[back_reach, my_group] = packed[my_group]
        pl.when(jnp.logical_not(waits_long))(prepare)
    else:
        pl.semaphore_wait(barrier, groups * stops - 1)
        for stop, group, peer in peers(-1):
            send(
                packed.at[group], received.at[stop, my_group], send_sem, recv_sems.at[stop],
                group, peer["rcv"],
            )
        received[back_reach, my_group] = packed[my_group]
        prepare()

    totals = [jnp.zeros((pairs, width), F32)] * freq_count
    for stop in reversed(far_first):
        arrived = received.at[stop]
        if stop == back_reach:
            arrived = received.at[stop, pl.ds(0, groups - 1)]
        pltpu.make_async_copy(arrived, arrived, recv_sems.at[stop]).wait()
        for group in range(groups):
            slots[stop, group * tile:group * tile + rows] = received[stop, group].astype(F32)
        regular = jnp.dot(
            mixers[...], slots[stop].astype(BF16), preferred_element_type=F32
        ).astype(BF16)
        for f in range(freq_count):
            at = 2 * f * pairs
            fields = jnp.concatenate(
                [regular[at:at + pairs], regular[at + pairs:at + 2 * pairs]], axis=1
            )
            totals[f] = totals[f] + jnp.dot(
                fields, operator[f, 2 * stop * width:2 * (stop + 1) * width],
                preferred_element_type=F32,
            )
    for f in range(freq_count):
        out_ref[f] = totals[f].astype(BF16)

    for stop in range(stops):
        sent = packed
        if stop == back_reach:
            sent = packed.at[pl.ds(0, groups - 1)]
        pltpu.make_async_copy(sent, sent, send_sem).wait()
    if relayed:
        @pl.when(my_panel == relay_panel)
        def _():
            pltpu.make_async_copy(relay, relay, relay_sems.at[1]).wait()


def shards(raw_blocks, raw_dest, raw_count, stencil, stencil_weight, kern):
    groups = lax.axis_size("acq")
    panels = lax.axis_size("rcv")
    stops = panels // 2
    raw_slots, sample_count, width = raw_blocks.shape
    freq_count = kern.shape[0]
    shot_count = stencil.shape[0]
    rows = 2 * freq_count
    tile = -(-rows // 8) * 8
    table = dft_table(freq_count, sample_count, -(-rows // 16) * 16)
    args = (table, raw_blocks, raw_dest, raw_count, stencil.T, stencil_weight.T, kern)
    out = pl.pallas_call(
        functools.partial(kernel, groups, panels, stops),
        out_shape=pltpu.VMEM((freq_count, 2 * shot_count, width), BF16),
        in_specs=[
            pl.BlockSpec(memory_space=pltpu.SMEM if arg is raw_count else pltpu.HBM)
            for arg in args
        ],
        out_specs=pl.BlockSpec(memory_space=pltpu.VMEM),
        scratch_shapes=[
            pltpu.VMEM(table.shape, BF16),
            pltpu.VMEM(raw_blocks.shape, BF16),
            pltpu.SMEM(raw_dest.shape, jnp.int32),
            pltpu.VMEM((2, shot_count), jnp.int32),
            pltpu.VMEM((2, shot_count), BF16),
            pltpu.VMEM(kern.shape, BF16),
            pltpu.VMEM((groups, rows, width), BF16),
            pltpu.VMEM((stops, groups, rows, width), BF16),
            pltpu.VMEM((groups, rows, width), BF16),
            pltpu.VMEM((stops, groups * tile, width), F32),
            pltpu.VMEM((2 * freq_count * 2 * shot_count, groups * tile), BF16),
            pltpu.VMEM((freq_count, 2 * stops * width, width), BF16),
            pltpu.SemaphoreType.DMA((raw_slots, 2)),
            pltpu.SemaphoreType.DMA((5,)),
            pltpu.SemaphoreType.DMA,
            pltpu.SemaphoreType.DMA((stops,)),
            pltpu.SemaphoreType.DMA((2,)),
        ],
        compiler_params=pltpu.CompilerParams(
            collective_id=0, has_side_effects=True, vmem_limit_bytes=32 * 1024 * 1024
        ),
    )(*(
        arg if arg is raw_count else pltpu.with_memory_space_constraint(arg, pltpu.HBM)
        for arg in args
    ))
    return out.reshape(freq_count, shot_count, 1, 2, width)


def solution(mesh):
    return jax.shard_map(
        shards,
        mesh=mesh,
        in_specs=(P("acq", None, "rcv"), P("acq"), P("acq"), P("acq", None), P("acq", None), P()),
        out_specs=P(None, "acq", "rcv", None, None),
        check_vma=False,
    )
```

```python
import functools
import math

import jax
import jax.numpy as jnp
import numpy as np
from jax import lax
from jax.experimental import pallas as pl
from jax.experimental.pallas import tpu as pltpu
from jax.sharding import PartitionSpec as P

FLO = 32
MESH = pl.DeviceIdType.MESH
F32 = jnp.float32
BF16 = jnp.bfloat16


def dft_table(freq_count, sample_count, row_count):
    freqs = FLO + np.arange(freq_count, dtype=np.int32)
    samples = np.arange(sample_count, dtype=np.int32)
    angles = (freqs[:, None] * samples[None, :] % sample_count).astype(np.float32) * np.float32(
        2.0 * math.pi / sample_count
    )
    rows = np.stack([np.cos(angles), -np.sin(angles)], axis=1) / np.float32(math.sqrt(sample_count))
    table = np.zeros((row_count, sample_count), np.float32)
    table[: 2 * freq_count] = rows.reshape(2 * freq_count, sample_count)
    return jnp.asarray(table, BF16)


def split(index, size):
    if size & (size - 1):
        return index // size, index % size
    return index >> (size.bit_length() - 1), index & (size - 1)


def kernel(
    groups, panels, stops,
    table_hbm, raw_hbm, dest_hbm, count_ref, stencil_hbm, weight_hbm, kern_hbm,
    out_ref,
    table, raw, dest, stencil, weight, kern, packed, received, relay, slots, mixers, operator,
    raw_sems, small_sems, send_sem, recv_sems, relay_sems,
):
    raw_slots, sample_count, width = raw.shape
    depth = sample_count // raw_sems.shape[1]
    freq_count = kern.shape[0]
    rows = 2 * freq_count
    tile = -(-rows // 8) * 8
    shot_count = stencil.shape[1]
    pairs = 2 * shot_count
    back_reach = stops // 2 - 1
    my_group = lax.axis_index("acq")
    my_panel = lax.axis_index("rcv")

    small = [
        pltpu.make_async_copy(src, dst, small_sems.at[at])
        for at, (src, dst) in enumerate([
            (dest_hbm, dest), (stencil_hbm, stencil), (weight_hbm, weight), (table_hbm, table),
            (kern_hbm, kern),
        ])
    ]
    loads = [
        [
            pltpu.make_async_copy(
                raw_hbm.at[j, pl.ds(first, depth)], raw.at[j, pl.ds(first, depth)],
                raw_sems.at[j, at],
            )
            for at, first in enumerate(range(0, sample_count, depth))
        ]
        for j in range(raw_slots)
    ]

    def moved(place, by, count):
        place = place + by
        if by < 0:
            return jnp.where(place < 0, place + count, place)
        return jnp.where(place >= count, place - count, place)

    if groups & (groups - 1):
        everyone = [moved(my_group, step, groups) for step in range(groups)]
    else:
        bits = range(groups.bit_length() - 1)
        flips = [(1 << bit) - (2 << bit) * (my_group // (1 << bit) % 2) for bit in bits]
        everyone = []
        for mask in sorted(range(groups), key=lambda mask: (-bin(mask >> 1).count("1"), -mask)):
            group = my_group
            for bit in bits:
                if mask >> bit & 1:
                    group = group + flips[bit]
            everyone.append(group)
        everyone = everyone[-1:] + everyone[:-1]
    others = everyone[1:]
    everyone = everyone[1:] + everyone[:1]

    far_first = sorted(range(stops), key=lambda stop: -abs(stop - back_reach))

    def peers(sign):
        for stop in far_first:
            panel = moved(my_panel, sign * (stop - back_reach), panels)
            for group in others if stop == back_reach else everyone:
                yield stop, group, {"acq": group, "rcv": panel}

    relayed = stops == 2 and panels >= 4
    last = panels - 1
    relay_panel = panels - 2
    barrier = pltpu.get_barrier_semaphore()

    def greet(group, panel):
        pl.semaphore_signal(
            barrier, inc=1, device_id={"acq": group, "rcv": panel}, device_id_type=MESH
        )

    if relayed:
        @pl.when(my_panel == relay_panel)
        def _():
            greet(my_group, 0)

        sender_panel = jnp.where(my_panel == last, relay_panel, my_panel + 1)
        for group in everyone:
            greet(group, sender_panel)
        for group in others:
            greet(group, my_panel)
    else:
        for _, group, peer in peers(1):
            greet(group, peer["rcv"])
    for block in loads:
        for load in block:
            load.start()
    for copy in small:
        copy.start()
    slots[...] = jnp.zeros_like(slots)
    small[0].wait()
    select_shape = (groups * tile, raw_slots * rows)
    owner_of, place_row = split(lax.broadcasted_iota(jnp.int32, select_shape, 0), tile)
    source, source_row = split(lax.broadcasted_iota(jnp.int32, select_shape, 1), rows)
    same_place = place_row == source_row
    target = jnp.full(select_shape, -1, jnp.int32)
    for j in range(raw_slots):
        target = jnp.where(source == j, jnp.where(j < count_ref[0], dest[j], -1), target)
    select = jnp.where(same_place & (owner_of == target), 1.0, 0.0).astype(BF16)

    def prepare():
        small[1].wait()
        small[2].wait()
        slot_at, _ = split(lax.broadcasted_iota(jnp.int32, (groups * tile, shot_count), 0), tile)
        weights = weight[...].astype(F32)
        mixing = jnp.where(slot_at == stencil[0:1, :], weights[0:1, :], 0.0)
        mixing = mixing + jnp.where(slot_at == stencil[1:2, :], weights[1:2, :], 0.0)
        spread_rows = lax.broadcasted_iota(jnp.int32, (pairs, shot_count), 0)
        spread_cols = lax.broadcasted_iota(jnp.int32, (pairs, shot_count), 1)
        spread = jnp.where(split(spread_rows, 2)[0] == spread_cols, 1.0, 0.0).astype(BF16)
        mixing = lax.dot_general(
            spread, mixing.astype(BF16), (((1,), (1,)), ((), ())), preferred_element_type=F32
        )
        _, part = split(lax.broadcasted_iota(jnp.int32, mixing.shape, 0), 2)
        signed = jnp.where(part == 0, mixing, -mixing)
        _, component = split(lax.broadcasted_iota(jnp.int32, mixing.shape, 1), tile)
        for f in range(freq_count):
            mixers[2 * f * pairs:(2 * f + 1) * pairs] = (
                jnp.where(component == 2 * f + part, mixing, 0.0).astype(BF16)
            )
            mixers[(2 * f + 1) * pairs:(2 * f + 2) * pairs] = (
                jnp.where(component == 2 * f + 1 - part, signed, 0.0).astype(BF16)
            )

        small[4].wait()
        lane = lax.broadcasted_iota(jnp.int32, (width, width), 1)
        row = lax.broadcasted_iota(jnp.int32, (width, width), 0)
        flip = jnp.where(lane + row == width - 1, 1.0, 0.0).astype(BF16)
        lines = jnp.concatenate([kern[f].astype(F32) for f in range(freq_count)], axis=0).astype(BF16)
        flipped = [
            jnp.dot(lines[:, at * width:(at + 1) * width], flip, preferred_element_type=F32)
            for at in range(stops + 1)
        ]
        for f in range(freq_count):
            for c in range(2):
                line = 2 * f + c
                rolled = []
                for at in range(stops + 1):
                    piece = flipped[at][line:line + 1]
                    piece = -piece if c == 1 else piece
                    rolled.append(pltpu.roll(
                        jnp.broadcast_to(piece, (width, width)), 1, 1, stride=1, stride_axis=0
                    ))
                for stop in range(stops):
                    place = (2 * stop + c) * width
                    operator[f, place:place + width] = jnp.where(
                        row >= lane, rolled[stop + 1], rolled[stop]
                    ).astype(BF16)

    if relayed:
        waits_long = (my_panel == 0) | (my_panel == relay_panel)
        pl.when(waits_long)(prepare)
    small[3].wait()
    pieces = []
    for first in range(0, raw_slots, 2):
        blocks = list(range(first, min(first + 2, raw_slots)))
        both = None
        for at in range(sample_count // depth):
            for j in blocks:
                loads[j][at].wait()
            span = slice(at * depth, (at + 1) * depth)
            term = jnp.dot(
                table[:, span], jnp.concatenate([raw[j, span] for j in blocks], axis=1),
                preferred_element_type=F32,
            )
            both = term if both is None else both + term
        for at in range(len(blocks)):
            pieces.append(both[:rows, at * width:(at + 1) * width])
    spectra = jnp.concatenate(pieces, axis=0).astype(BF16)
    gathered = jnp.dot(select, spectra, preferred_element_type=F32)
    for owner in range(groups):
        packed[owner] = gathered[owner * tile:owner * tile + rows].astype(BF16)

    def send(src, dst, send_to, recv_to, group, panel):
        pltpu.make_async_remote_copy(
            src_ref=src, dst_ref=dst, send_sem=send_to, recv_sem=recv_to,
            device_id={"acq": group, "rcv": panel}, device_id_type=MESH,
        ).start()

    if relayed:
        @pl.when(my_panel == 0)
        def _():
            pl.semaphore_wait(barrier, groups)
            send(packed, relay, send_sem, relay_sems.at[0], my_group, relay_panel)

        @pl.when(my_panel == relay_panel)
        def _():
            pl.semaphore_wait(barrier, 3 * groups - 1)

        @pl.when((my_panel == last) | ((my_panel > 0) & (my_panel < relay_panel)))
        def _():
            pl.semaphore_wait(barrier, 2 * groups - 1)

        @pl.when(my_panel > 0)
        def _():
            for group in everyone:
                send(
                    packed.at[group], received.at[1, my_group], send_sem, recv_sems.at[1],
                    group, my_panel - 1,
                )

        for group in others:
            send(
                packed.at[group], received.at[0, my_group], send_sem, recv_sems.at[0],
                group, my_panel,
            )

        @pl.when(my_panel == relay_panel)
        def _():
            pltpu.make_async_copy(relay, relay, relay_sems.at[0]).wait()
            for group in everyone:
                send(
                    relay.at[group], received.at[1, my_group], relay_sems.at[1], recv_sems.at[1],
                    group, last,
                )

        received[back_reach, my_group] = packed[my_group]
        pl.when(jnp.logical_not(waits_long))(prepare)
    else:
        pl.semaphore_wait(barrier, groups * stops - 1)
        for stop, group, peer in peers(-1):
            send(
                packed.at[group], received.at[stop, my_group], send_sem, recv_sems.at[stop],
                group, peer["rcv"],
            )
        received[back_reach, my_group] = packed[my_group]
        prepare()

    totals = [jnp.zeros((pairs, width), F32)] * freq_count
    for stop in reversed(far_first):
        arrived = received.at[stop]
        if stop == back_reach:
            arrived = received.at[stop, pl.ds(0, groups - 1)]
        pltpu.make_async_copy(arrived, arrived, recv_sems.at[stop]).wait()
        for group in range(groups):
            slots[stop, group * tile:group * tile + rows] = received[stop, group].astype(F32)
        regular = jnp.dot(
            mixers[...], slots[stop].astype(BF16), preferred_element_type=F32
        ).astype(BF16)
        for f in range(freq_count):
            at = 2 * f * pairs
            fields = jnp.concatenate(
                [regular[at:at + pairs], regular[at + pairs:at + 2 * pairs]], axis=1
            )
            totals[f] = totals[f] + jnp.dot(
                fields, operator[f, 2 * stop * width:2 * (stop + 1) * width],
                preferred_element_type=F32,
            )
    for f in range(freq_count):
        out_ref[f] = totals[f].astype(BF16)

    for stop in range(stops):
        sent = packed
        if stop == back_reach:
            sent = packed.at[pl.ds(0, groups - 1)]
        pltpu.make_async_copy(sent, sent, send_sem).wait()
    if relayed:
        @pl.when(my_panel == relay_panel)
        def _():
            pltpu.make_async_copy(relay, relay, relay_sems.at[1]).wait()


def shards(raw_blocks, raw_dest, raw_count, stencil, stencil_weight, kern):
    groups = lax.axis_size("acq")
    panels = lax.axis_size("rcv")
    stops = panels // 2
    raw_slots, sample_count, width = raw_blocks.shape
    freq_count = kern.shape[0]
    shot_count = stencil.shape[0]
    rows = 2 * freq_count
    tile = -(-rows // 8) * 8
    table = dft_table(freq_count, sample_count, -(-rows // 16) * 16)
    args = (table, raw_blocks, raw_dest, raw_count, stencil.T, stencil_weight.T, kern)
    out = pl.pallas_call(
        functools.partial(kernel, groups, panels, stops),
        out_shape=pltpu.VMEM((freq_count, 2 * shot_count, width), BF16),
        in_specs=[
            pl.BlockSpec(memory_space=pltpu.SMEM if arg is raw_count else pltpu.HBM)
            for arg in args
        ],
        out_specs=pl.BlockSpec(memory_space=pltpu.VMEM),
        scratch_shapes=[
            pltpu.VMEM(table.shape, BF16),
            pltpu.VMEM(raw_blocks.shape, BF16),
            pltpu.SMEM(raw_dest.shape, jnp.int32),
            pltpu.VMEM((2, shot_count), jnp.int32),
            pltpu.VMEM((2, shot_count), BF16),
            pltpu.VMEM(kern.shape, BF16),
            pltpu.VMEM((groups, rows, width), BF16),
            pltpu.VMEM((stops, groups, rows, width), BF16),
            pltpu.VMEM((groups, rows, width), BF16),
            pltpu.VMEM((stops, groups * tile, width), F32),
            pltpu.VMEM((2 * freq_count * 2 * shot_count, groups * tile), BF16),
            pltpu.VMEM((freq_count, 2 * stops * width, width), BF16),
            pltpu.SemaphoreType.DMA((raw_slots, 2)),
            pltpu.SemaphoreType.DMA((5,)),
            pltpu.SemaphoreType.DMA,
            pltpu.SemaphoreType.DMA((stops,)),
            pltpu.SemaphoreType.DMA((2,)),
        ],
        compiler_params=pltpu.CompilerParams(
            collective_id=0, has_side_effects=True, vmem_limit_bytes=32 * 1024 * 1024
        ),
    )(*(
        arg if arg is raw_count else pltpu.with_memory_space_constraint(arg, pltpu.HBM)
        for arg in args
    ))
    return out.reshape(freq_count, shot_count, 1, 2, width)


def solution(mesh):
    return jax.shard_map(
        shards,
        mesh=mesh,
        in_specs=(P("acq", None, "rcv"), P("acq"), P("acq"), P("acq", None), P("acq", None), P()),
        out_specs=P(None, "acq", "rcv", None, None),
        check_vma=False,
    )
```

```python
import functools
import math

import jax
import jax.numpy as jnp
import numpy as np
from jax import lax
from jax.experimental import pallas as pl
from jax.experimental.pallas import tpu as pltpu
from jax.sharding import PartitionSpec as P

FLO = 32
MESH = pl.DeviceIdType.MESH
F32 = jnp.float32
BF16 = jnp.bfloat16


def dft_table(freq_count, sample_count, row_count):
    freqs = FLO + np.arange(freq_count, dtype=np.int32)
    samples = np.arange(sample_count, dtype=np.int32)
    angles = (freqs[:, None] * samples[None, :] % sample_count).astype(np.float32) * np.float32(
        2.0 * math.pi / sample_count
    )
    rows = np.stack([np.cos(angles), -np.sin(angles)], axis=1) / np.float32(math.sqrt(sample_count))
    table = np.zeros((row_count, sample_count), np.float32)
    table[: 2 * freq_count] = rows.reshape(2 * freq_count, sample_count)
    return jnp.asarray(table, BF16)


def split(index, size):
    if size & (size - 1):
        return index // size, index % size
    return index >> (size.bit_length() - 1), index & (size - 1)


def kernel(
    groups, panels, stops,
    table_hbm, raw_hbm, dest_hbm, count_ref, stencil_hbm, weight_hbm, kern_hbm,
    out_ref,
    table, raw, dest, stencil, weight, kern, packed, received, relay, slots, mixers, operator,
    raw_sems, small_sems, send_sem, recv_sems, relay_sems,
):
    raw_slots, sample_count, width = raw.shape
    depth = sample_count // raw_sems.shape[1]
    freq_count = kern.shape[0]
    rows = 2 * freq_count
    tile = -(-rows // 8) * 8
    shot_count = stencil.shape[1]
    pairs = 2 * shot_count
    back_reach = stops // 2 - 1
    my_group = lax.axis_index("acq")
    my_panel = lax.axis_index("rcv")

    small = [
        pltpu.make_async_copy(src, dst, small_sems.at[at])
        for at, (src, dst) in enumerate([
            (dest_hbm, dest), (stencil_hbm, stencil), (weight_hbm, weight), (table_hbm, table),
            (kern_hbm, kern),
        ])
    ]
    loads = [
        [
            pltpu.make_async_copy(
                raw_hbm.at[j, pl.ds(first, depth)], raw.at[j, pl.ds(first, depth)],
                raw_sems.at[j, at],
            )
            for at, first in enumerate(range(0, sample_count, depth))
        ]
        for j in range(raw_slots)
    ]

    def moved(place, by, count):
        place = place + by
        if by < 0:
            return jnp.where(place < 0, place + count, place)
        return jnp.where(place >= count, place - count, place)

    if groups & (groups - 1):
        everyone = [moved(my_group, step, groups) for step in range(groups)]
    else:
        bits = range(groups.bit_length() - 1)
        flips = [(1 << bit) - (2 << bit) * (my_group // (1 << bit) % 2) for bit in bits]
        everyone = []
        for mask in sorted(range(groups), key=lambda mask: (-bin(mask >> 1).count("1"), -mask)):
            group = my_group
            for bit in bits:
                if mask >> bit & 1:
                    group = group + flips[bit]
            everyone.append(group)
        everyone = everyone[-1:] + everyone[:-1]
    others = everyone[1:]
    everyone = everyone[1:] + everyone[:1]

    far_first = sorted(range(stops), key=lambda stop: -abs(stop - back_reach))

    def peers(sign):
        for stop in far_first:
            panel = moved(my_panel, sign * (stop - back_reach), panels)
            for group in others if stop == back_reach else everyone:
                yield stop, group, {"acq": group, "rcv": panel}

    relayed = stops == 2 and panels >= 4
    last = panels - 1
    relay_panel = panels - 2
    barrier = pltpu.get_barrier_semaphore()

    def greet(group, panel):
        pl.semaphore_signal(
            barrier, inc=1, device_id={"acq": group, "rcv": panel}, device_id_type=MESH
        )

    if relayed:
        @pl.when(my_panel == relay_panel)
        def _():
            greet(my_group, 0)

    for block in loads:
        for load in block:
            load.start()

    if relayed:
        sender_panel = jnp.where(my_panel == last, relay_panel, my_panel + 1)
        for group in everyone:
            greet(group, sender_panel)
        for group in others:
            greet(group, my_panel)
    else:
        for _, group, peer in peers(1):
            greet(group, peer["rcv"])
    for copy in small:
        copy.start()
    slots[...] = jnp.zeros_like(slots)
    small[0].wait()
    select_shape = (groups * tile, raw_slots * rows)
    owner_of, place_row = split(lax.broadcasted_iota(jnp.int32, select_shape, 0), tile)
    source, source_row = split(lax.broadcasted_iota(jnp.int32, select_shape, 1), rows)
    same_place = place_row == source_row
    target = jnp.full(select_shape, -1, jnp.int32)
    for j in range(raw_slots):
        target = jnp.where(source == j, jnp.where(j < count_ref[0], dest[j], -1), target)
    select = jnp.where(same_place & (owner_of == target), 1.0, 0.0).astype(BF16)

    def prepare():
        small[1].wait()
        small[2].wait()
        slot_at, _ = split(lax.broadcasted_iota(jnp.int32, (groups * tile, shot_count), 0), tile)
        weights = weight[...].astype(F32)
        mixing = jnp.where(slot_at == stencil[0:1, :], weights[0:1, :], 0.0)
        mixing = mixing + jnp.where(slot_at == stencil[1:2, :], weights[1:2, :], 0.0)
        spread_rows = lax.broadcasted_iota(jnp.int32, (pairs, shot_count), 0)
        spread_cols = lax.broadcasted_iota(jnp.int32, (pairs, shot_count), 1)
        spread = jnp.where(split(spread_rows, 2)[0] == spread_cols, 1.0, 0.0).astype(BF16)
        mixing = lax.dot_general(
            spread, mixing.astype(BF16), (((1,), (1,)), ((), ())), preferred_element_type=F32
        )
        _, part = split(lax.broadcasted_iota(jnp.int32, mixing.shape, 0), 2)
        signed = jnp.where(part == 0, mixing, -mixing)
        _, component = split(lax.broadcasted_iota(jnp.int32, mixing.shape, 1), tile)
        for f in range(freq_count):
            mixers[2 * f * pairs:(2 * f + 1) * pairs] = (
                jnp.where(component == 2 * f + part, mixing, 0.0).astype(BF16)
            )
            mixers[(2 * f + 1) * pairs:(2 * f + 2) * pairs] = (
                jnp.where(component == 2 * f + 1 - part, signed, 0.0).astype(BF16)
            )

        small[4].wait()
        lane = lax.broadcasted_iota(jnp.int32, (width, width), 1)
        row = lax.broadcasted_iota(jnp.int32, (width, width), 0)
        flip = jnp.where(lane + row == width - 1, 1.0, 0.0).astype(BF16)
        lines = jnp.concatenate([kern[f].astype(F32) for f in range(freq_count)], axis=0).astype(BF16)
        flipped = [
            jnp.dot(lines[:, at * width:(at + 1) * width], flip, preferred_element_type=F32)
            for at in range(stops + 1)
        ]
        for f in range(freq_count):
            for c in range(2):
                line = 2 * f + c
                rolled = []
                for at in range(stops + 1):
                    piece = flipped[at][line:line + 1]
                    piece = -piece if c == 1 else piece
                    rolled.append(pltpu.roll(
                        jnp.broadcast_to(piece, (width, width)), 1, 1, stride=1, stride_axis=0
                    ))
                for stop in range(stops):
                    place = (2 * stop + c) * width
                    operator[f, place:place + width] = jnp.where(
                        row >= lane, rolled[stop + 1], rolled[stop]
                    ).astype(BF16)

    if relayed:
        waits_long = (my_panel == 0) | (my_panel == relay_panel)
        pl.when(waits_long)(prepare)
    small[3].wait()
    pieces = []
    for first in range(0, raw_slots, 2):
        blocks = list(range(first, min(first + 2, raw_slots)))
        both = None
        for at in range(sample_count // depth):
            for j in blocks:
                loads[j][at].wait()
            span = slice(at * depth, (at + 1) * depth)
            term = jnp.dot(
                table[:, span], jnp.concatenate([raw[j, span] for j in blocks], axis=1),
                preferred_element_type=F32,
            )
            both = term if both is None else both + term
        for at in range(len(blocks)):
            pieces.append(both[:rows, at * width:(at + 1) * width])
    spectra = jnp.concatenate(pieces, axis=0).astype(BF16)
    gathered = jnp.dot(select, spectra, preferred_element_type=F32)
    for owner in range(groups):
        packed[owner] = gathered[owner * tile:owner * tile + rows].astype(BF16)

    def send(src, dst, send_to, recv_to, group, panel):
        pltpu.make_async_remote_copy(
            src_ref=src, dst_ref=dst, send_sem=send_to, recv_sem=recv_to,
            device_id={"acq": group, "rcv": panel}, device_id_type=MESH,
        ).start()

    if relayed:
        @pl.when(my_panel == 0)
        def _():
            pl.semaphore_wait(barrier, groups)
            send(packed, relay, send_sem, relay_sems.at[0], my_group, relay_panel)

        @pl.when(my_panel == relay_panel)
        def _():
            pl.semaphore_wait(barrier, 3 * groups - 1)

        @pl.when((my_panel == last) | ((my_panel > 0) & (my_panel < relay_panel)))
        def _():
            pl.semaphore_wait(barrier, 2 * groups - 1)

        @pl.when(my_panel > 0)
        def _():
            for group in everyone:
                send(
                    packed.at[group], received.at[1, my_group], send_sem, recv_sems.at[1],
                    group, my_panel - 1,
                )

        for group in others:
            send(
                packed.at[group], received.at[0, my_group], send_sem, recv_sems.at[0],
                group, my_panel,
            )

        @pl.when(my_panel == relay_panel)
        def _():
            pltpu.make_async_copy(relay, relay, relay_sems.at[0]).wait()
            for group in everyone:
                send(
                    relay.at[group], received.at[1, my_group], relay_sems.at[1], recv_sems.at[1],
                    group, last,
                )

        received[back_reach, my_group] = packed[my_group]
        pl.when(jnp.logical_not(waits_long))(prepare)
    else:
        pl.semaphore_wait(barrier, groups * stops - 1)
        for stop, group, peer in peers(-1):
            send(
                packed.at[group], received.at[stop, my_group], send_sem, recv_sems.at[stop],
                group, peer["rcv"],
            )
        received[back_reach, my_group] = packed[my_group]
        prepare()

    totals = [jnp.zeros((pairs, width), F32)] * freq_count
    for stop in reversed(far_first):
        arrived = received.at[stop]
        if stop == back_reach:
            arrived = received.at[stop, pl.ds(0, groups - 1)]
        pltpu.make_async_copy(arrived, arrived, recv_sems.at[stop]).wait()
        for group in range(groups):
            slots[stop, group * tile:group * tile + rows] = received[stop, group].astype(F32)
        regular = jnp.dot(
            mixers[...], slots[stop].astype(BF16), preferred_element_type=F32
        ).astype(BF16)
        for f in range(freq_count):
            at = 2 * f * pairs
            fields = jnp.concatenate(
                [regular[at:at + pairs], regular[at + pairs:at + 2 * pairs]], axis=1
            )
            totals[f] = totals[f] + jnp.dot(
                fields, operator[f, 2 * stop * width:2 * (stop + 1) * width],
                preferred_element_type=F32,
            )
    for f in range(freq_count):
        out_ref[f] = totals[f].astype(BF16)

    for stop in range(stops):
        sent = packed
        if stop == back_reach:
            sent = packed.at[pl.ds(0, groups - 1)]
        pltpu.make_async_copy(sent, sent, send_sem).wait()
    if relayed:
        @pl.when(my_panel == relay_panel)
        def _():
            pltpu.make_async_copy(relay, relay, relay_sems.at[1]).wait()


def shards(raw_blocks, raw_dest, raw_count, stencil, stencil_weight, kern):
    groups = lax.axis_size("acq")
    panels = lax.axis_size("rcv")
    stops = panels // 2
    raw_slots, sample_count, width = raw_blocks.shape
    freq_count = kern.shape[0]
    shot_count = stencil.shape[0]
    rows = 2 * freq_count
    tile = -(-rows // 8) * 8
    table = dft_table(freq_count, sample_count, -(-rows // 16) * 16)
    args = (table, raw_blocks, raw_dest, raw_count, stencil.T, stencil_weight.T, kern)
    out = pl.pallas_call(
        functools.partial(kernel, groups, panels, stops),
        out_shape=pltpu.VMEM((freq_count, 2 * shot_count, width), BF16),
        in_specs=[
            pl.BlockSpec(memory_space=pltpu.SMEM if arg is raw_count else pltpu.HBM)
            for arg in args
        ],
        out_specs=pl.BlockSpec(memory_space=pltpu.VMEM),
        scratch_shapes=[
            pltpu.VMEM(table.shape, BF16),
            pltpu.VMEM(raw_blocks.shape, BF16),
            pltpu.SMEM(raw_dest.shape, jnp.int32),
            pltpu.VMEM((2, shot_count), jnp.int32),
            pltpu.VMEM((2, shot_count), BF16),
            pltpu.VMEM(kern.shape, BF16),
            pltpu.VMEM((groups, rows, width), BF16),
            pltpu.VMEM((stops, groups, rows, width), BF16),
            pltpu.VMEM((groups, rows, width), BF16),
            pltpu.VMEM((stops, groups * tile, width), F32),
            pltpu.VMEM((2 * freq_count * 2 * shot_count, groups * tile), BF16),
            pltpu.VMEM((freq_count, 2 * stops * width, width), BF16),
            pltpu.SemaphoreType.DMA((raw_slots, 2)),
            pltpu.SemaphoreType.DMA((5,)),
            pltpu.SemaphoreType.DMA,
            pltpu.SemaphoreType.DMA((stops,)),
            pltpu.SemaphoreType.DMA((2,)),
        ],
        compiler_params=pltpu.CompilerParams(
            collective_id=0, has_side_effects=True, vmem_limit_bytes=32 * 1024 * 1024
        ),
    )(*(
        arg if arg is raw_count else pltpu.with_memory_space_constraint(arg, pltpu.HBM)
        for arg in args
    ))
    return out.reshape(freq_count, shot_count, 1, 2, width)


def solution(mesh):
    return jax.shard_map(
        shards,
        mesh=mesh,
        in_specs=(P("acq", None, "rcv"), P("acq"), P("acq"), P("acq", None), P("acq", None), P()),
        out_specs=P(None, "acq", "rcv", None, None),
        check_vma=False,
    )
```

```python
import functools
import math

import jax
import jax.numpy as jnp
import numpy as np
from jax import lax
from jax.experimental import pallas as pl
from jax.experimental.pallas import tpu as pltpu
from jax.sharding import PartitionSpec as P

FLO = 32
MESH = pl.DeviceIdType.MESH
F32 = jnp.float32
BF16 = jnp.bfloat16


def dft_table(freq_count, sample_count, row_count):
    freqs = FLO + np.arange(freq_count, dtype=np.int32)
    samples = np.arange(sample_count, dtype=np.int32)
    angles = (freqs[:, None] * samples[None, :] % sample_count).astype(np.float32) * np.float32(
        2.0 * math.pi / sample_count
    )
    rows = np.stack([np.cos(angles), -np.sin(angles)], axis=1) / np.float32(math.sqrt(sample_count))
    table = np.zeros((row_count, sample_count), np.float32)
    table[: 2 * freq_count] = rows.reshape(2 * freq_count, sample_count)
    return jnp.asarray(table, BF16)


def split(index, size):
    if size & (size - 1):
        return index // size, index % size
    return index >> (size.bit_length() - 1), index & (size - 1)


def kernel(
    groups, panels, stops,
    table_hbm, raw_hbm, dest_hbm, count_ref, stencil_hbm, weight_hbm, kern_hbm,
    out_ref,
    table, raw, dest, stencil, weight, kern, packed, received, relay, slots, mixers, operator,
    raw_sems, small_sems, send_sem, recv_sems, relay_sems,
):
    raw_slots, sample_count, width = raw.shape
    depth = sample_count // raw_sems.shape[1]
    freq_count = kern.shape[0]
    rows = 2 * freq_count
    tile = -(-rows // 8) * 8
    shot_count = stencil.shape[1]
    pairs = 2 * shot_count
    back_reach = stops // 2 - 1
    my_group = lax.axis_index("acq")
    my_panel = lax.axis_index("rcv")

    small = [
        pltpu.make_async_copy(src, dst, small_sems.at[at])
        for at, (src, dst) in enumerate([
            (dest_hbm, dest), (stencil_hbm, stencil), (weight_hbm, weight), (table_hbm, table),
            (kern_hbm, kern),
        ])
    ]
    loads = [
        [
            pltpu.make_async_copy(
                raw_hbm.at[j, pl.ds(first, depth)], raw.at[j, pl.ds(first, depth)],
                raw_sems.at[j, at],
            )
            for at, first in enumerate(range(0, sample_count, depth))
        ]
        for j in range(raw_slots)
    ]

    def moved(place, by, count):
        place = place + by
        if by < 0:
            return jnp.where(place < 0, place + count, place)
        return jnp.where(place >= count, place - count, place)

    if groups & (groups - 1):
        everyone = [moved(my_group, step, groups) for step in range(groups)]
    else:
        bits = range(groups.bit_length() - 1)
        flips = [(1 << bit) - (2 << bit) * (my_group // (1 << bit) % 2) for bit in bits]
        everyone = []
        for mask in sorted(range(groups), key=lambda mask: (-bin(mask >> 1).count("1"), -mask)):
            group = my_group
            for bit in bits:
                if mask >> bit & 1:
                    group = group + flips[bit]
            everyone.append(group)
        everyone = everyone[-1:] + everyone[:-1]
    others = everyone[1:]
    everyone = everyone[1:] + everyone[:1]

    far_first = sorted(range(stops), key=lambda stop: -abs(stop - back_reach))

    def peers(sign):
        for stop in far_first:
            panel = moved(my_panel, sign * (stop - back_reach), panels)
            for group in others if stop == back_reach else everyone:
                yield stop, group, {"acq": group, "rcv": panel}

    relayed = stops == 2 and panels >= 4
    last = panels - 1
    relay_panel = panels - 2
    barrier = pltpu.get_barrier_semaphore()

    def greet(group, panel):
        pl.semaphore_signal(
            barrier, inc=1, device_id={"acq": group, "rcv": panel}, device_id_type=MESH
        )

    if relayed:
        @pl.when(my_panel == relay_panel)
        def _():
            greet(my_group, 0)

    for block in loads:
        for load in block:
            load.start()

    if relayed:
        sender_panel = jnp.where(my_panel == last, relay_panel, my_panel + 1)
        for group in everyone:
            greet(group, sender_panel)
        for group in others:
            greet(group, my_panel)
    else:
        for _, group, peer in peers(1):
            greet(group, peer["rcv"])
    for copy in small:
        copy.start()
    slots[...] = jnp.zeros_like(slots)
    small[0].wait()
    select_shape = (groups * tile, raw_slots * rows)
    owner_of, place_row = split(lax.broadcasted_iota(jnp.int32, select_shape, 0), tile)
    source, source_row = split(lax.broadcasted_iota(jnp.int32, select_shape, 1), rows)
    same_place = place_row == source_row
    target = jnp.full(select_shape, -1, jnp.int32)
    for j in range(raw_slots):
        target = jnp.where(source == j, jnp.where(j < count_ref[0], dest[j], -1), target)
    select = jnp.where(same_place & (owner_of == target), 1.0, 0.0).astype(BF16)

    def prepare():
        small[1].wait()
        small[2].wait()
        slot_at, _ = split(lax.broadcasted_iota(jnp.int32, (groups * tile, shot_count), 0), tile)
        weights = weight[...].astype(F32)
        mixing = jnp.where(slot_at == stencil[0:1, :], weights[0:1, :], 0.0)
        mixing = mixing + jnp.where(slot_at == stencil[1:2, :], weights[1:2, :], 0.0)
        spread_rows = lax.broadcasted_iota(jnp.int32, (pairs, shot_count), 0)
        spread_cols = lax.broadcasted_iota(jnp.int32, (pairs, shot_count), 1)
        spread = jnp.where(split(spread_rows, 2)[0] == spread_cols, 1.0, 0.0).astype(BF16)
        mixing = lax.dot_general(
            spread, mixing.astype(BF16), (((1,), (1,)), ((), ())), preferred_element_type=F32
        )
        _, part = split(lax.broadcasted_iota(jnp.int32, mixing.shape, 0), 2)
        signed = jnp.where(part == 0, mixing, -mixing)
        _, component = split(lax.broadcasted_iota(jnp.int32, mixing.shape, 1), tile)
        for f in range(freq_count):
            mixers[2 * f * pairs:(2 * f + 1) * pairs] = (
                jnp.where(component == 2 * f + part, mixing, 0.0).astype(BF16)
            )
            mixers[(2 * f + 1) * pairs:(2 * f + 2) * pairs] = (
                jnp.where(component == 2 * f + 1 - part, signed, 0.0).astype(BF16)
            )

        small[4].wait()
        lane = lax.broadcasted_iota(jnp.int32, (width, width), 1)
        row = lax.broadcasted_iota(jnp.int32, (width, width), 0)
        flip = jnp.where(lane + row == width - 1, 1.0, 0.0).astype(BF16)
        lines = jnp.concatenate([kern[f].astype(F32) for f in range(freq_count)], axis=0).astype(BF16)
        flipped = [
            jnp.dot(lines[:, at * width:(at + 1) * width], flip, preferred_element_type=F32)
            for at in range(stops + 1)
        ]
        for f in range(freq_count):
            for c in range(2):
                line = 2 * f + c
                rolled = []
                for at in range(stops + 1):
                    piece = flipped[at][line:line + 1]
                    piece = -piece if c == 1 else piece
                    rolled.append(pltpu.roll(
                        jnp.broadcast_to(piece, (width, width)), 1, 1, stride=1, stride_axis=0
                    ))
                for stop in range(stops):
                    place = (2 * stop + c) * width
                    operator[f, place:place + width] = jnp.where(
                        row >= lane, rolled[stop + 1], rolled[stop]
                    ).astype(BF16)

    if relayed:
        waits_long = (my_panel == 0) | (my_panel == relay_panel)
        pl.when(waits_long)(prepare)
    small[3].wait()
    pieces = []
    for first in range(0, raw_slots, 2):
        blocks = list(range(first, min(first + 2, raw_slots)))
        both = None
        for at in range(sample_count // depth):
            for j in blocks:
                loads[j][at].wait()
            span = slice(at * depth, (at + 1) * depth)
            term = jnp.dot(
                table[:, span], jnp.concatenate([raw[j, span] for j in blocks], axis=1),
                preferred_element_type=F32,
            )
            both = term if both is None else both + term
        for at in range(len(blocks)):
            pieces.append(both[:rows, at * width:(at + 1) * width])
    spectra = jnp.concatenate(pieces, axis=0).astype(BF16)
    gathered = jnp.dot(select, spectra, preferred_element_type=F32)
    for owner in range(groups):
        packed[owner] = gathered[owner * tile:owner * tile + rows].astype(BF16)

    def send(src, dst, send_to, recv_to, group, panel):
        pltpu.make_async_remote_copy(
            src_ref=src, dst_ref=dst, send_sem=send_to, recv_sem=recv_to,
            device_id={"acq": group, "rcv": panel}, device_id_type=MESH,
        ).start()

    if relayed:
        @pl.when(my_panel == 0)
        def _():
            pl.semaphore_wait(barrier, groups)
            send(packed, relay, send_sem, relay_sems.at[0], my_group, relay_panel)

        @pl.when(my_panel == relay_panel)
        def _():
            pl.semaphore_wait(barrier, 3 * groups - 1)

        @pl.when((my_panel == last) | ((my_panel > 0) & (my_panel < relay_panel)))
        def _():
            pl.semaphore_wait(barrier, 2 * groups - 1)

        @pl.when(my_panel > 0)
        def _():
            for group in everyone:
                send(
                    packed.at[group], received.at[1, my_group], send_sem, recv_sems.at[1],
                    group, my_panel - 1,
                )

        for group in others:
            send(
                packed.at[group], received.at[0, my_group], send_sem, recv_sems.at[0],
                group, my_panel,
            )

        @pl.when(my_panel == relay_panel)
        def _():
            pltpu.make_async_copy(relay, relay, relay_sems.at[0]).wait()
            for group in everyone:
                send(
                    relay.at[group], received.at[1, my_group], relay_sems.at[1], recv_sems.at[1],
                    group, last,
                )

        received[back_reach, my_group] = packed[my_group]
        pl.when(jnp.logical_not(waits_long))(prepare)
    else:
        pl.semaphore_wait(barrier, groups * stops - 1)
        for stop, group, peer in peers(-1):
            send(
                packed.at[group], received.at[stop, my_group], send_sem, recv_sems.at[stop],
                group, peer["rcv"],
            )
        received[back_reach, my_group] = packed[my_group]
        prepare()

    totals = [jnp.zeros((pairs, width), F32)] * freq_count
    for stop in reversed(far_first):
        arrived = received.at[stop]
        if stop == back_reach:
            arrived = received.at[stop, pl.ds(0, groups - 1)]
        pltpu.make_async_copy(arrived, arrived, recv_sems.at[stop]).wait()
        for group in range(groups):
            slots[stop, group * tile:group * tile + rows] = received[stop, group].astype(F32)
        regular = jnp.dot(
            mixers[...], slots[stop].astype(BF16), preferred_element_type=F32
        ).astype(BF16)
        for f in range(freq_count):
            at = 2 * f * pairs
            fields = jnp.concatenate(
                [regular[at:at + pairs], regular[at + pairs:at + 2 * pairs]], axis=1
            )
            totals[f] = totals[f] + jnp.dot(
                fields, operator[f, 2 * stop * width:2 * (stop + 1) * width],
                preferred_element_type=F32,
            )
    for f in range(freq_count):
        out_ref[f] = totals[f].astype(BF16)

    for stop in range(stops):
        sent = packed
        if stop == back_reach:
            sent = packed.at[pl.ds(0, groups - 1)]
        pltpu.make_async_copy(sent, sent, send_sem).wait()
    if relayed:
        @pl.when(my_panel == relay_panel)
        def _():
            pltpu.make_async_copy(relay, relay, relay_sems.at[1]).wait()


def shards(raw_blocks, raw_dest, raw_count, stencil, stencil_weight, kern):
    groups = lax.axis_size("acq")
    panels = lax.axis_size("rcv")
    stops = panels // 2
    raw_slots, sample_count, width = raw_blocks.shape
    freq_count = kern.shape[0]
    shot_count = stencil.shape[0]
    rows = 2 * freq_count
    tile = -(-rows // 8) * 8
    table = dft_table(freq_count, sample_count, -(-rows // 16) * 16)
    args = (table, raw_blocks, raw_dest, raw_count, stencil.T, stencil_weight.T, kern)
    out = pl.pallas_call(
        functools.partial(kernel, groups, panels, stops),
        out_shape=pltpu.VMEM((freq_count, 2 * shot_count, width), BF16),
        in_specs=[
            pl.BlockSpec(memory_space=pltpu.SMEM if arg is raw_count else pltpu.HBM)
            for arg in args
        ],
        out_specs=pl.BlockSpec(memory_space=pltpu.VMEM),
        scratch_shapes=[
            pltpu.VMEM(table.shape, BF16),
            pltpu.VMEM(raw_blocks.shape, BF16),
            pltpu.SMEM(raw_dest.shape, jnp.int32),
            pltpu.VMEM((2, shot_count), jnp.int32),
            pltpu.VMEM((2, shot_count), BF16),
            pltpu.VMEM(kern.shape, BF16),
            pltpu.VMEM((groups, rows, width), BF16),
            pltpu.VMEM((stops, groups, rows, width), BF16),
            pltpu.VMEM((groups, rows, width), BF16),
            pltpu.VMEM((stops, groups * tile, width), F32),
            pltpu.VMEM((2 * freq_count * 2 * shot_count, groups * tile), BF16),
            pltpu.VMEM((freq_count, 2 * stops * width, width), BF16),
            pltpu.SemaphoreType.DMA((raw_slots, 1)),
            pltpu.SemaphoreType.DMA((5,)),
            pltpu.SemaphoreType.DMA,
            pltpu.SemaphoreType.DMA((stops,)),
            pltpu.SemaphoreType.DMA((2,)),
        ],
        compiler_params=pltpu.CompilerParams(
            collective_id=0, has_side_effects=True, vmem_limit_bytes=32 * 1024 * 1024
        ),
    )(*(
        arg if arg is raw_count else pltpu.with_memory_space_constraint(arg, pltpu.HBM)
        for arg in args
    ))
    return out.reshape(freq_count, shot_count, 1, 2, width)


def solution(mesh):
    return jax.shard_map(
        shards,
        mesh=mesh,
        in_specs=(P("acq", None, "rcv"), P("acq"), P("acq"), P("acq", None), P("acq", None), P()),
        out_specs=P(None, "acq", "rcv", None, None),
        check_vma=False,
    )
```
